128 devices in a mesh: tm: 8 (over y, x_lo), feat: 16 (over x_hi, z, core).
Axes of the slice: x: 4 (x_hi: 2, x_lo: 2; x = x_hi * 2 + x_lo), y: 4, z: 4, core: 2. Of those that a mesh axis runs over, the one named last changes fastest.
Arguments:
- frames: float32 [4096, 8192], P('tm', 'feat'), may hold values from -15 to 25, as said below
Outputs:
- instant: float32 [8192, 8192], P('tm', 'feat')
- lagged: float32 [8192, 8192], P('tm', 'feat')
The draws below stay inside these ranges and needn't reach their ends.
Inputs may be any that keep to these rules, and one draw needn't show every extreme that they name: `frames`: real-valued feature values.
All inputs are finite; a program needn't handle non-finite values.
Results may differ from the reference program's by a relative error of at most 0.0003.
Values sent between devices are 32-bit elements; how exact they have to be, the bound alone decides.
No kernel may reach another device: no remote copies, remote signals or barrier semaphores. Data moves between devices by JAX's collectives and lax.ppermute only.
A program may use at most 128 MiB of HBM per device.

```python
import math
import jax
import jax.numpy as jnp
from jax import lax

FEAT = 8192
LAG = 100
FRAMES = 4096


def draw_frames(key, part):
    key = jax.random.fold_in(key, 11)
    keys = jax.random.split(key, 8)
    noise = jnp.clip(jax.random.normal(keys[0], (FRAMES, FEAT), jnp.float32), -4.0, 4.0)
    offsets = jax.random.uniform(keys[1], (1, FEAT), jnp.float32, 2.0, 6.0)
    row_scale = jnp.exp(jax.random.uniform(keys[2], (FRAMES, 1), jnp.float32, math.log(0.3), math.log(3.0)))
    col_scale = jnp.exp(jax.random.uniform(keys[3], (1, FEAT), jnp.float32, math.log(0.3), math.log(1.0)))
    period = jax.random.uniform(keys[4], (1, FEAT), jnp.float32, 150.0, 2000.0)
    phase = jax.random.uniform(keys[7], (1, FEAT), jnp.float32, -3.14159, 3.14159)
    times = jnp.arange(FRAMES, dtype=jnp.float32)[:, None]
    slow = jnp.sin(times * (6.2831853 / period) + phase)
    return offsets + row_scale * col_scale * noise + slow


def setup_inputs(seed: int = 0) -> dict:
    splits = jax.random.split(jax.random.key(seed), 2)
    frames = draw_frames(jax.random.fold_in(splits[1], 71), 0)
    return {"frames": frames}


def reference(frames):
    column_mean = jnp.mean(frames, axis=0)
    centred = frames - column_mean
    instant = jnp.dot(centred.T, centred, precision=lax.Precision.HIGHEST, preferred_element_type=jnp.float32) / FRAMES
    lagged = jnp.dot(centred[:FRAMES - LAG].T, centred[LAG:], precision=lax.Precision.HIGHEST, preferred_element_type=jnp.float32) / (FRAMES - LAG)
    return instant, lagged
```

```python
import jax
import jax.numpy as jnp
from jax import lax
from jax.sharding import PartitionSpec as P

LAG = 100
AXES = ("tm", "feat")
DEVICES = 128


def place(device):
    tm, feat = divmod(device, 16)
    return feat // 8, tm % 2, tm // 2, feat // 2 % 4, feat % 2


def device_at(x_hi, x_lo, y, z, core):
    return (y % 4 * 2 + x_lo) * 16 + (x_hi * 4 + z % 4) * 2 + core


def move(block, step):
    route = [(d, device_at(*step(*place(d)))) for d in range(DEVICES)]
    return lax.ppermute(block, AXES, route)


def along_x_lo(block):
    return move(block, lambda xh, xl, y, z, c: (xh, 1 - xl, y, z, c))


def along_x_hi(block):
    return move(block, lambda xh, xl, y, z, c: (1 - xh, xl, y, z, c))


def along_y(block, n):
    return move(block, lambda xh, xl, y, z, c: (xh, xl, y + n, z, c))


def along_z(block, n):
    return move(block, lambda xh, xl, y, z, c: (xh, xl, y, z + n, c))


def other_core(block):
    return move(block, lambda xh, xl, y, z, c: (xh, xl, y, z, 1 - c))


def pair_in_plane(turn, y):
    return 2 * (turn // 2 ^ y // 2) + (turn % 2 ^ y % 2)


def to_row_owner(block, turn):
    def step(xh, xl, y, z, c):
        pair = pair_in_plane(turn, y)
        return xh ^ pair // 2 ^ xl, pair % 2, 2 * xh + pair // 2, z, c

    return move(block, step)


def gather_columns(own):
    rows = own.shape[0]
    half = rows // 2
    tm = lax.axis_index("tm")
    y, x_lo = tm // 2, tm % 2
    other = along_x_lo(own)
    whole = jnp.zeros((8 * rows, own.shape[1]), own.dtype)

    def put(whole, block, y_from, x_from, skip=0):
        at = (lax.rem(y_from + 4, 4) * 2 + x_from) * rows + skip
        return lax.dynamic_update_slice(whole, block, (at, 0))

    for block, x_from in ((own, x_lo), (other, 1 - x_lo)):
        below, above = along_y(block, 1), along_y(block, -1)
        far_low, far_high = along_y(below[:half], 1), along_y(above[half:], -1)
        whole = put(whole, block, y, x_from)
        whole = put(whole, below, y - 1, x_from)
        whole = put(whole, above, y + 1, x_from)
        whole = put(whole, far_low, y - 2, x_from)
        whole = put(whole, far_high, y + 2, x_from, half)
    return whole


def gather_rows(own):
    rows, width = own.shape
    y, z = lax.axis_index("tm") // 2, lax.axis_index("feat") // 2 % 4
    quarters = own.T.reshape(4, width // 4, rows)
    spread = jnp.stack([quarters[0]] + [along_z(quarters[n], n) for n in (1, 2, 3)])
    landed, swapped = [], []
    for turn in range(4):
        which = lax.rem(z - pair_in_plane(turn, y) + 4, 4)
        block = to_row_owner(lax.dynamic_index_in_dim(spread, which, 0, keepdims=False), turn)
        landed.append(block)
        swapped.append(along_x_hi(block))
    near = jnp.stack([landed[0], swapped[0], landed[1], swapped[1]])
    late = jnp.stack([landed[2], swapped[2], landed[3], swapped[3]])
    below = along_z(near, 1), along_z(late, 1)
    above = along_z(near, -1), along_z(late, -1)
    far = along_z(below[0], 1), along_z(above[1], -1)
    return (near, late), below, above, far


def on_device(frames):
    rows, width = frames.shape
    tm, feat = lax.axis_index("tm"), lax.axis_index("feat")
    y, x_lo, x_hi, z, core = tm // 2, tm % 2, feat // 8, feat // 2 % 4, feat % 2
    total = 8 * rows
    quarter = width // 4

    columns = gather_columns(frames)
    columns = columns - jnp.mean(columns, axis=0)
    padded = jnp.concatenate([columns, jnp.zeros((LAG, width), columns.dtype)])
    ordered = []
    x_first = x_hi ^ y // 2 ^ y % 2
    for turn in range(4):
        y_from = 2 * (y % 2 ^ turn // 2) + (x_lo ^ turn % 2)
        for x_from in (x_first, 1 - x_first):
            at = (2 * y_from + x_from) * rows
            now = lax.dynamic_slice(padded, (at, 0), (rows, width))
            later = lax.dynamic_slice(padded, (at + LAG, 0), (rows, width))
            ordered.append(jnp.concatenate([now, later], axis=1))
    ordered = jnp.stack(ordered)

    instant = jnp.zeros((2 * width, width), frames.dtype)
    lagged = instant
    first = z - (y % 2 * 2 + x_lo)
    for chunk, away in zip(gather_rows(frames), (0, -1, 1, 2)):
        mine = jnp.concatenate(chunk)
        theirs = other_core(mine)
        at = lax.rem(first + away + 8, 4) * quarter
        for block, whose in ((mine, core), (theirs, 1 - core)):
            block = block - jnp.mean(block, axis=(0, 2), keepdims=True)
            product = lax.dot_general(
                block,
                ordered,
                (((0, 2), (0, 1)), ((), ())),
                precision=lax.Precision.HIGH,
                preferred_element_type=jnp.float32,
            )
            row = whose * width + at
            instant = lax.dynamic_update_slice(instant, product[:, :width] / total, (row, 0))
            lagged = lax.dynamic_update_slice(lagged, product[:, width:] / (total - LAG), (row, 0))
    return instant, lagged


def solution(mesh):
    return jax.shard_map(
        on_device,
        mesh=mesh,
        in_specs=(P("tm", "feat"),),
        out_specs=(P("tm", "feat"), P("tm", "feat")),
        check_vma=False,
    )
```

```python
import functools

import jax
import jax.numpy as jnp
from jax import lax
from jax.experimental import pallas as pl
from jax.experimental.pallas import tpu as pltpu
from jax.sharding import PartitionSpec as P

LAG = 100
AXES = ("tm", "feat")
DEVICES = 128
SLOTS = 8
VMEM = 40 * 2**20


def place(device):
    tm, feat = divmod(device, 16)
    return feat // 8, tm % 2, tm // 2, feat // 2 % 4, feat % 2


def device_at(x_hi, x_lo, y, z, core):
    return (y % 4 * 2 + x_lo) * 16 + (x_hi * 4 + z % 4) * 2 + core


def move(block, step):
    route = [(d, device_at(*step(*place(d)))) for d in range(DEVICES)]
    return lax.ppermute(block, AXES, route)


def along_x_lo(block):
    return move(block, lambda xh, xl, y, z, c: (xh, 1 - xl, y, z, c))


def along_x_hi(block):
    return move(block, lambda xh, xl, y, z, c: (1 - xh, xl, y, z, c))


def along_y(block, n):
    return move(block, lambda xh, xl, y, z, c: (xh, xl, y + n, z, c))


def along_z(block, n):
    return move(block, lambda xh, xl, y, z, c: (xh, xl, y, z + n, c))


def other_core(block):
    return move(block, lambda xh, xl, y, z, c: (xh, xl, y, z, 1 - c))


def pair_in_plane(turn, y):
    return 2 * (turn // 2 ^ y // 2) + (turn % 2 ^ y % 2)


def to_row_owner(block, turn):
    def step(xh, xl, y, z, c):
        pair = pair_in_plane(turn, y)
        return xh ^ pair // 2 ^ xl, pair % 2, 2 * xh + pair // 2, z, c

    return move(block, step)


together = lax.optimization_barrier


def split(x):
    high = x.astype(jnp.bfloat16)
    return high, (x - high.astype(jnp.float32)).astype(jnp.bfloat16)


def columns_kernel(sizes, first, rows_ref, *refs):
    n = len(sizes)
    pieces, refs = refs[:n], refs[n:]
    if first:
        high_out, low_out, centre_out, sums_out, high, low, sems = refs
        block = pieces[0][...]
        centre = jnp.sum(block, axis=0, keepdims=True) / block.shape[0]
        centre_out[...] = centre
        sums = jnp.zeros_like(centre)
    else:
        centre_in, sums_in, _, _, high_out, low_out, sums_out, high, low, sems = refs
        centre, sums = centre_in[...], sums_in[...]
    copies, at = [], 0
    for i, size in enumerate(sizes):
        block = pieces[i][...] - centre
        sums = sums + jnp.sum(block, axis=0, keepdims=True)
        here = pl.ds(at, size)
        high[here, :], low[here, :] = split(block)
        there = pl.ds(pl.multiple_of(rows_ref[i], 128), size)
        for j, (held, out) in enumerate(((high, high_out), (low, low_out))):
            copy = pltpu.make_async_copy(held.at[here], out.at[there], sems.at[2 * i + j])
            copy.start()
            copies.append(copy)
        at += size
    sums_out[...] = sums
    for copy in copies:
        copy.wait()


def split_columns(pieces, starts, total, state=None):
    sizes = [p.shape[0] for p in pieces]
    width = pieces[0].shape[1]
    n, first = len(pieces), state is None
    whole = jax.ShapeDtypeStruct((total, width), jnp.bfloat16)
    line = jax.ShapeDtypeStruct((1, width), jnp.float32)
    anywhere = pl.BlockSpec(memory_space=pl.ANY)
    held = pl.BlockSpec(memory_space=pltpu.VMEM)
    more, more_specs, aliases = [], [], {}
    if not first:
        high, low, centre, sums = state
        more, more_specs = [centre, sums, high, low], [held, held, anywhere, anywhere]
        aliases = {n + 3: 0, n + 4: 1}
    count = sum(sizes) * width
    out = pl.pallas_call(
        functools.partial(columns_kernel, sizes, first),
        grid_spec=pltpu.PrefetchScalarGridSpec(
            num_scalar_prefetch=1,
            grid=(),
            in_specs=[held] * n + more_specs,
            out_specs=[anywhere, anywhere] + [held] * (2 if first else 1),
            scratch_shapes=[
                pltpu.VMEM((sum(sizes), width), jnp.bfloat16),
                pltpu.VMEM((sum(sizes), width), jnp.bfloat16),
                pltpu.SemaphoreType.DMA((2 * n,)),
            ],
        ),
        out_shape=[whole, whole] + [line] * (2 if first else 1),
        input_output_aliases=aliases,
        cost_estimate=pl.CostEstimate(flops=6 * count, bytes_accessed=8 * count, transcendentals=0),
        compiler_params=pltpu.CompilerParams(vmem_limit_bytes=VMEM),
        name="split_columns",
    )(jnp.stack(starts).astype(jnp.int32), *pieces, *more)
    if first:
        return out
    return out[0], out[1], state[2], out[2]


def rows_kernel(facts_ref, *refs):
    pieces, (high_out, low_out, edge_out, held) = refs[:4], refs[4:]
    step = pl.program_id(0)
    count, rows, frames = pieces[0].shape

    @pl.when(step == 0)
    def _():
        for half in range(2):
            near, late = pieces[2 * half], pieces[2 * half + 1]
            total = jnp.zeros((rows, frames), jnp.float32)
            for i in range(count):
                total = total + (near[i] + late[i])
            mean = jnp.sum(total, axis=1, keepdims=True) / (2 * count * frames)
            core = facts_ref[0] if half == 0 else 1 - facts_ref[0]
            there = pl.ds(pl.multiple_of(core * rows, rows), rows)
            for i in range(count):
                held[i, there, :] = near[i] - mean
                held[count + i, there, :] = late[i] - mean
        edge_out[...] = jnp.zeros_like(edge_out)

    now = held[step]
    before = held[facts_ref[1 + step]]
    before = jnp.where(facts_ref[1 + SLOTS + step] == 0, 0.0, before)
    lane = lax.broadcasted_iota(jnp.int32, now.shape, 1)
    shifted = jnp.where(lane < LAG, pltpu.roll(before, LAG, 1), pltpu.roll(now, LAG, 1))
    edge_out[...] += jnp.sum(shifted, axis=1, keepdims=True)
    high_out[0, : 2 * rows], low_out[0, : 2 * rows] = split(now)
    high_out[0, 2 * rows :], low_out[0, 2 * rows :] = split(shifted)


def split_rows(near, late, near_other, late_other, facts):
    count, rows, frames = near.shape
    whole = jax.ShapeDtypeStruct((SLOTS, 4 * rows, frames), jnp.bfloat16)
    once = pl.BlockSpec((count, rows, frames), lambda s, f: (0, 0, 0), pipeline_mode=pl.Buffered(1))
    each = pl.BlockSpec((1, 4 * rows, frames), lambda s, f: (s, 0, 0))
    size = SLOTS * 2 * rows * frames
    return pl.pallas_call(
        rows_kernel,
        grid_spec=pltpu.PrefetchScalarGridSpec(
            num_scalar_prefetch=1,
            grid=(SLOTS,),
            in_specs=[once] * 4,
            out_specs=[each, each, pl.BlockSpec((2 * rows, 128), lambda s, f: (0, 0))],
            scratch_shapes=[pltpu.VMEM((SLOTS, 2 * rows, frames), jnp.float32)],
        ),
        out_shape=[whole, whole, jax.ShapeDtypeStruct((2 * rows, 128), jnp.float32)],
        cost_estimate=pl.CostEstimate(flops=10 * size, bytes_accessed=12 * size, transcendentals=0),
        compiler_params=pltpu.CompilerParams(vmem_limit_bytes=VMEM),
        name="split_rows",
    )(facts, near, late, near_other, late_other)


def product_kernel(first, facts_ref, ah, al, edge, bh, bl, sums, *refs):
    instant_out, lagged_out, total = refs if first else refs[2:]
    step = pl.program_id(0)
    dot = functools.partial(jnp.dot, preferred_element_type=jnp.float32)
    high, low, right = ah[0], al[0], bh[0]
    part = dot(high, right) + dot(low, right) + dot(high, bl[0])

    @pl.when(step == 0)
    def _():
        total[...] = part

    @pl.when((step > 0) & (step < SLOTS - 1))
    def _():
        total[...] += part

    @pl.when(step == SLOTS - 1)
    def _():
        done = total[...] + part
        rows = done.shape[0] // 2
        frames = SLOTS * high.shape[1]
        off = sums[...] / frames
        instant_out[...] = (done[:rows] / frames).reshape(instant_out.shape)
        lagged = (done[rows:] - edge[:, :1] * off) / (frames - LAG)
        lagged_out[...] = lagged.reshape(lagged_out.shape)


def product(rows, columns, facts, outs):
    ah, al, edge = rows
    bh, bl, _, sums = columns
    _, m, frames = ah.shape
    width = bh.shape[1]
    quarter = m // 4
    bh, bl = (b.reshape(SLOTS, frames, width) for b in (bh, bl))
    left = pl.BlockSpec((1, m, frames), lambda s, f: (s, 0, 0))
    right = pl.BlockSpec((1, frames, width), lambda s, f: (f[1 + s], 0, 0))
    out = pl.BlockSpec((2, 1, quarter, width), lambda s, f: (0, f[0], 0, 0))
    shape = jax.ShapeDtypeStruct((2, 4, quarter, width), jnp.float32)
    first = outs is None
    more = () if first else outs
    flops = 2 * 3 * SLOTS * m * frames * width
    return pl.pallas_call(
        functools.partial(product_kernel, first),
        grid_spec=pltpu.PrefetchScalarGridSpec(
            num_scalar_prefetch=1,
            grid=(SLOTS,),
            in_specs=[
                left,
                left,
                pl.BlockSpec((2 * quarter, 128), lambda s, f: (0, 0)),
                right,
                right,
                pl.BlockSpec((1, width), lambda s, f: (0, 0)),
            ]
            + [pl.BlockSpec(memory_space=pl.ANY)] * len(more),
            out_specs=[out, out],
            scratch_shapes=[pltpu.VMEM((m, width), jnp.float32)],
        ),
        out_shape=[shape, shape],
        input_output_aliases={} if first else {7: 0, 8: 1},
        cost_estimate=pl.CostEstimate(
            flops=flops, bytes_accessed=4 * SLOTS * frames * (m + width), transcendentals=0
        ),
        compiler_params=pltpu.CompilerParams(vmem_limit_bytes=VMEM),
        name="product",
    )(facts, ah, al, edge, bh, bl, sums, *more)


def on_device(frames):
    rows, width = frames.shape
    half, fourth = rows // 2, rows // 4
    quarter = width // 4
    total = SLOTS * rows
    tm, feat = lax.axis_index("tm"), lax.axis_index("feat")
    y, x_lo, x_hi, z, core = tm // 2, tm % 2, feat // 8, feat // 2 % 4, feat % 2

    own = frames
    quarters = own.T.reshape(4, quarter, rows)
    spread = [quarters[0]] + [along_z(quarters[n], n) for n in (1, 2, 3)]
    below1, above1 = along_y(own[:half], 1), along_y(own[:half], -1)
    other1 = along_x_lo(own[:half])
    *spread, below1, above1, other1 = together((*spread, below1, above1, other1))

    spread = jnp.stack(spread)
    landed = []
    for turn in range(4):
        which = lax.rem(z - pair_in_plane(turn, y) + 4, 4)
        landed.append(to_row_owner(lax.dynamic_index_in_dim(spread, which, 0, keepdims=False), turn))
    *landed, own = together((*landed, own))

    swapped = [along_x_hi(landed[0]), along_x_hi(landed[1])]
    below2, above2 = along_y(own[half:], 1), along_y(own[half:], -1)
    *swapped, below2, above2, own, late1, late2, other1 = together((*swapped, below2, above2, own, *landed[2:], other1))

    near = jnp.stack([landed[0], swapped[0], landed[1], swapped[1]])
    swapped = [along_x_hi(late1), along_x_hi(late2)]
    other2 = along_x_lo(own[half:])
    below_near, above_near = along_z(near, 1), along_z(near, -1)
    far1, far2 = along_y(below1, 1), along_y(above2, -1)
    cross_below1, cross_above1 = along_y(other1, 1), along_y(other1, -1)
    *swapped, other2, near, below_near, above_near, far1, far2, cross_below1, cross_above1 = together(
        (*swapped, other2, near, below_near, above_near, far1, far2, cross_below1, cross_above1)
    )

    late = jnp.stack([late1, swapped[0], late2, swapped[1]])
    below_late, above_late = along_z(late, 1), along_z(late, -1)
    cross_below2, cross_above2 = along_y(other2, 1), along_y(other2, -1)
    cross_far1, cross_far2 = along_y(cross_below1[:fourth], 1), along_y(cross_above1[fourth:], -1)
    near_other, below_near_other, above_near_other = (other_core(b) for b in (near, below_near, above_near))
    late, below_late, above_late, below_near, above_near, cross_below2, cross_above2, cross_far1, cross_far2 = together(
        (late, below_late, above_late, below_near, above_near, cross_below2, cross_above2, cross_far1, cross_far2)
    )

    far_near, far_late = along_z(below_near, 1), along_z(above_late, -1)
    cross_far3, cross_far4 = along_y(cross_below2[:fourth], 1), along_y(cross_above2[fourth:], -1)
    late_other, below_late_other, above_late_other = (other_core(b) for b in (late, below_late, above_late))
    far_near_other, far_late_other = other_core(far_near), other_core(far_late)

    def start(y_off, x_from, skip):
        return (lax.rem(y + y_off + 4, 4) * 2 + x_from) * rows + skip

    here, cross = x_lo, 1 - x_lo
    columns = split_columns(
        [own, other1, other2, below1, below2, above1, above2, far1, far2, cross_below1, cross_above1, cross_far1, cross_far2],
        [
            start(0, here, 0),
            start(0, cross, 0),
            start(0, cross, half),
            start(-1, here, 0),
            start(-1, here, half),
            start(1, here, 0),
            start(1, here, half),
            start(-2, here, 0),
            start(2, here, half),
            start(-1, cross, 0),
            start(1, cross, 0),
            start(-2, cross, 0),
            start(2, cross, fourth),
        ],
        total,
    )
    columns = split_columns(
        [cross_below2, cross_above2, cross_far3, cross_far4],
        [start(-1, cross, half), start(1, cross, half), start(-2, cross, half), start(2, cross, half + fourth)],
        total,
        columns,
    )

    times = []
    x_first = x_hi ^ y // 2 ^ y % 2
    for turn in range(4):
        y_from = 2 * (y % 2 ^ turn // 2) + (x_lo ^ turn % 2)
        times += [2 * y_from + x_first, 2 * y_from + 1 - x_first]
    times = jnp.stack(times).astype(jnp.int32)
    before = jnp.argmax(times[None, :] == jnp.maximum(times - 1, 0)[:, None], axis=1).astype(jnp.int32)
    row_facts = jnp.concatenate([core.astype(jnp.int32)[None], before, times])
    first = z - (y % 2 * 2 + x_lo)

    def facts(away):
        return jnp.concatenate([lax.rem(first + away + 8, 4).astype(jnp.int32)[None], times])

    outs = None
    for away, parts in (
        (0, (near, late, near_other, late_other)),
        (-1, (below_near, below_late, below_near_other, below_late_other)),
        (1, (above_near, above_late, above_near_other, above_late_other)),
        (2, (far_near, far_late, far_near_other, far_late_other)),
    ):
        outs = product(split_rows(*parts, row_facts), columns, facts(away), outs)
    return tuple(out.reshape(2 * width, width) for out in outs)


def solution(mesh):
    return jax.shard_map(
        on_device,
        mesh=mesh,
        in_specs=(P("tm", "feat"),),
        out_specs=(P("tm", "feat"), P("tm", "feat")),
        check_vma=False,
    )
```

```python
import functools

import jax
import jax.numpy as jnp
from jax import lax
from jax.experimental import pallas as pl
from jax.experimental.pallas import tpu as pltpu
from jax.sharding import PartitionSpec as P

LAG = 100
AXES = ("tm", "feat")
DEVICES = 128
SLOTS = 8
VMEM = 32 * 2**20
SPACE = pltpu.HBM
FACTS = {"core": 0, "times": 1, "order": 9, "chunks": 17}


def place(device):
    tm, feat = divmod(device, 16)
    return feat // 8, tm % 2, tm // 2, feat // 2 % 4, feat % 2


def device_at(x_hi, x_lo, y, z, core):
    return (y % 4 * 2 + x_lo) * 16 + (x_hi * 4 + z % 4) * 2 + core


def move(block, step):
    route = [(d, device_at(*step(*place(d)))) for d in range(DEVICES)]
    return lax.ppermute(block, AXES, route)


def along_x_lo(block):
    return move(block, lambda xh, xl, y, z, c: (xh, 1 - xl, y, z, c))


def along_x_hi(block):
    return move(block, lambda xh, xl, y, z, c: (1 - xh, xl, y, z, c))


def along_y(block, n):
    return move(block, lambda xh, xl, y, z, c: (xh, xl, y + n, z, c))


def along_z(block, n):
    return move(block, lambda xh, xl, y, z, c: (xh, xl, y, z + n, c))


def other_core(block):
    return move(block, lambda xh, xl, y, z, c: (xh, xl, y, z, 1 - c))


def together(*blocks):
    return lax.optimization_barrier(blocks)


def pair_in_plane(turn, y):
    return 2 * (turn // 2 ^ y // 2) + (turn % 2 ^ y % 2)


def to_row_owner(block, turn):
    def step(xh, xl, y, z, c):
        pair = pair_in_plane(turn, y)
        return xh ^ pair // 2 ^ xl, pair % 2, 2 * xh + pair // 2, z, c

    return move(block, step)


def split(x):
    high = x.astype(jnp.bfloat16)
    return high, (x - high.astype(jnp.float32)).astype(jnp.bfloat16)


def columns_kernel(sizes, skip, first, facts_ref, *refs):
    n = len(sizes)
    pieces, refs = refs[:n], refs[n:]
    if first:
        high_out, low_out, centre_out, sums_out, raw, high, low, sems = refs
    else:
        centre_in, sums_in, _, _, high_out, low_out, sums_out, raw, high, low, sems = refs
    size = sizes[0]
    loads = [pltpu.make_async_copy(piece, raw.at[i], sems.at[2 * n + i]) for i, piece in enumerate(pieces)]
    for load in loads:
        load.start()
    copies = []
    for i in range(n):
        loads[i].wait()
        block = raw[i]
        if first and i == 0:
            centre = jnp.sum(block, axis=0, keepdims=True) / size
            centre_out[...] = centre
            sums = jnp.zeros_like(centre)
        elif i == 0:
            centre, sums = centre_in[...], sums_in[...]
        block = block - centre
        sums = sums + jnp.sum(block, axis=0, keepdims=True)
        high[i], low[i] = split(block)
        there = pl.ds(pl.multiple_of(facts_ref[FACTS["order"] + skip + i] * size, size), size)
        for j, (held, out) in enumerate(((high, high_out), (low, low_out))):
            copy = pltpu.make_async_copy(held.at[i], out.at[there], sems.at[2 * i + j])
            copy.start()
            copies.append(copy)
    sums_out[...] = sums
    for copy in copies:
        copy.wait()


def split_columns(pieces, skip, facts, total, state=None):
    sizes = [p.shape[0] for p in pieces]
    width = pieces[0].shape[1]
    n, first = len(pieces), state is None
    whole = jax.ShapeDtypeStruct((total, width), jnp.bfloat16)
    line = jax.ShapeDtypeStruct((1, width), jnp.float32)
    anywhere = pl.BlockSpec(memory_space=SPACE)
    held = pl.BlockSpec(memory_space=pltpu.VMEM)
    more, more_specs, aliases = [], [], {}
    if not first:
        high, low, centre, sums = state
        more, more_specs = [centre, sums, high, low], [held, held, anywhere, anywhere]
        aliases = {n + 3: 0, n + 4: 1}
    count = sum(sizes) * width
    out = pl.pallas_call(
        functools.partial(columns_kernel, sizes, skip, first),
        grid_spec=pltpu.PrefetchScalarGridSpec(
            num_scalar_prefetch=1,
            grid=(),
            in_specs=[anywhere] * n + more_specs,
            out_specs=[anywhere, anywhere] + [held] * (2 if first else 1),
            scratch_shapes=[
                pltpu.VMEM((n, sizes[0], width), jnp.float32),
                pltpu.VMEM((n, sizes[0], width), jnp.bfloat16),
                pltpu.VMEM((n, sizes[0], width), jnp.bfloat16),
                pltpu.SemaphoreType.DMA((3 * n,)),
            ],
        ),
        out_shape=[whole, whole] + [line] * (2 if first else 1),
        input_output_aliases=aliases,
        cost_estimate=pl.CostEstimate(flops=6 * count, bytes_accessed=8 * count, transcendentals=0),
        compiler_params=pltpu.CompilerParams(vmem_limit_bytes=VMEM),
        name="split_columns",
    )(facts, *pieces, *more)
    if first:
        return out
    return out[0], out[1], state[2], out[2]


def start_columns(facts_ref, pairs, sources, held, sems):
    copies = []
    size = held[0].shape[1] // 2
    for n, pair in enumerate(pairs):
        for i in range(2):
            row = facts_ref[FACTS["order"] + 2 * pair + i] * size
            for j in range(2):
                copies.append(
                    pltpu.make_async_copy(
                        sources[j].at[pl.ds(pl.multiple_of(row, size), size)],
                        held[j].at[n, pl.ds(i * size, size)],
                        sems.at[4 * n + 2 * i + j],
                    )
                )
                copies[-1].start()
    return copies


def write_out(facts_ref, total, edge, sums, count, outs, done, parts, sems):
    rows = total.shape[0] // 4
    done[0] = total[: 2 * rows] / count
    done[1] = (total[2 * rows :] - edge * (sums / count)) / (count - LAG)
    copies = []
    for i, out in enumerate(outs):
        for half in range(2):
            there = out.at[half, facts_ref[FACTS["chunks"] + parts]]
            here = done.at[i, pl.ds(half * rows, rows)]
            copies.append(pltpu.make_async_copy(here, there, sems.at[2 * i + half]))
            copies[-1].start()
    return copies


dot = functools.partial(jnp.dot, preferred_element_type=jnp.float32)


def chunk_kernel(part, ready, facts_ref, *refs):
    last = ready == 4
    pieces, (bh_in, bl_in), refs = refs[:4], refs[4:6], refs[6:]
    if last:
        sums, _, _, instant_out, lagged_out, raw, held, bh, bl, total, done, sems = refs
    else:
        total, edge_out, high_out, low_out, raw, held, bh, bl, sems = refs
    groups, rows, frames = pieces[0].shape

    a_copies = [pltpu.make_async_copy(p, raw.at[i], sems.at[i]) for i, p in enumerate(pieces)]
    for copy in a_copies:
        copy.start()
    b_copies = start_columns(facts_ref, range(ready), (bh_in, bl_in), (bh, bl), sems.at[pl.ds(4, 16)])

    for half in range(2):
        a_copies[2 * half].wait()
        a_copies[2 * half + 1].wait()
        sum_ = jnp.zeros((rows, frames), jnp.float32)
        for g in range(groups):
            sum_ = sum_ + (raw[2 * half, g] + raw[2 * half + 1, g])
        mean = jnp.sum(sum_, axis=1, keepdims=True) / (2 * groups * frames)
        core = facts_ref[FACTS["core"]]
        core = core if half == 0 else 1 - core
        there = pl.ds(pl.multiple_of(core * rows, rows), rows)
        for i in range(2):
            for g in range(groups):
                held[facts_ref[FACTS["times"] + 2 * g + i], there, :] = raw[2 * half + i, g] - mean

    edge = jnp.zeros((2 * rows, 1), jnp.float32)
    lane = lax.broadcasted_iota(jnp.int32, (2 * rows, frames), 1)
    for pair in range(4):
        now, shifted = [], []
        for i in range(2):
            time = facts_ref[FACTS["order"] + 2 * pair + i]
            now.append(held[time])
            before = held[jnp.maximum(time - 1, 0)]
            before = jnp.where(time == 0, 0.0, before)
            moved = jnp.where(lane < LAG, pltpu.roll(before, LAG, 1), pltpu.roll(now[i], LAG, 1))
            edge = edge + jnp.sum(moved, axis=1, keepdims=True)
            shifted.append(moved)
        both = [jnp.concatenate(blocks, axis=1) for blocks in (now, shifted)]
        high, low = split(jnp.concatenate(both, axis=0))
        if pair >= ready:
            high_out[pair - ready], low_out[pair - ready] = high, low
            continue
        for copy in b_copies[4 * pair : 4 * pair + 4]:
            copy.wait()
        product = dot(high, bh[pair]) + dot(low, bh[pair]) + dot(high, bl[pair])
        if pair == 0:
            total[...] = product
        else:
            total[...] += product
    if last:
        copies = write_out(
            facts_ref, total, edge, sums[...], 2 * groups * frames, (instant_out, lagged_out), done, part, sems
        )
        for copy in copies:
            copy.wait()
    else:
        edge_out[...] = jnp.broadcast_to(edge, edge_out.shape)


def finish_kernel(parts, facts_ref, *refs):
    n = len(parts)
    begun, (bh_in, bl_in, sums, instant_out, lagged_out), refs = refs[: 4 * n], refs[4 * n : 4 * n + 5], refs[4 * n + 5 :]
    bh, bl, done, sems = refs
    late = [begun[4 * i + 2].shape[0] for i in range(n)]
    pairs = range(4 - max(late), 4)
    b_copies = start_columns(facts_ref, pairs, (bh_in, bl_in), (bh, bl), sems.at[pl.ds(4 * n, 4 * len(pairs))])
    for copy in b_copies:
        copy.wait()
    copies = []
    for i, part in enumerate(parts):
        total, edge, high, low = begun[4 * i : 4 * i + 4]
        now = total[...]
        for j in range(late[i]):
            k = j + max(late) - late[i]
            now = now + (dot(high[j], bh[k]) + dot(low[j], bh[k]) + dot(high[j], bl[k]))
        count = 4 * high.shape[2]
        copies += write_out(
            facts_ref, now, edge[:, :1], sums[...], count, (instant_out, lagged_out), done.at[i], part, sems.at[pl.ds(4 * i, 4)]
        )
    for copy in copies:
        copy.wait()


def begin(part, ready, pieces, columns, facts):
    bh, bl = columns[:2]
    groups, rows, frames = pieces[0].shape
    width, run = bh.shape[1], 2 * frames
    anywhere = pl.BlockSpec(memory_space=SPACE)
    held = pl.BlockSpec(memory_space=pltpu.VMEM)
    return pl.pallas_call(
        functools.partial(chunk_kernel, part, ready),
        grid_spec=pltpu.PrefetchScalarGridSpec(
            num_scalar_prefetch=1,
            grid=(),
            in_specs=[anywhere] * 6,
            out_specs=[held] * 4,
            scratch_shapes=[
                pltpu.VMEM((4, groups, rows, frames), jnp.float32),
                pltpu.VMEM((SLOTS, 2 * rows, frames), jnp.float32),
                pltpu.VMEM((ready, run, width), jnp.bfloat16),
                pltpu.VMEM((ready, run, width), jnp.bfloat16),
                pltpu.SemaphoreType.DMA((20,)),
            ],
        ),
        out_shape=[
            jax.ShapeDtypeStruct((4 * rows, width), jnp.float32),
            jax.ShapeDtypeStruct((2 * rows, 128), jnp.float32),
            jax.ShapeDtypeStruct((4 - ready, 4 * rows, run), jnp.bfloat16),
            jax.ShapeDtypeStruct((4 - ready, 4 * rows, run), jnp.bfloat16),
        ],
        cost_estimate=pl.CostEstimate(
            flops=2 * 3 * 4 * rows * ready * run * width, bytes_accessed=4 * groups * run * (2 * rows + width), transcendentals=0
        ),
        compiler_params=pltpu.CompilerParams(vmem_limit_bytes=VMEM),
        name="begin",
    )(facts, *pieces, bh, bl)


def finish(parts, begun, columns, facts):
    bh, bl, _, sums = columns
    rows, width = begun[0][1].shape[0] // 2, bh.shape[1]
    run = begun[0][2].shape[2]
    late = [chunk[2].shape[0] for chunk in begun]
    anywhere = pl.BlockSpec(memory_space=SPACE)
    held = pl.BlockSpec(memory_space=pltpu.VMEM)
    shape = jax.ShapeDtypeStruct((2, 4, rows, width), jnp.float32)
    n = len(parts)
    return pl.pallas_call(
        functools.partial(finish_kernel, parts),
        grid_spec=pltpu.PrefetchScalarGridSpec(
            num_scalar_prefetch=1,
            grid=(),
            in_specs=[held] * (4 * n) + [anywhere] * 2 + [held],
            out_specs=[anywhere, anywhere],
            scratch_shapes=[
                pltpu.VMEM((max(late), run, width), jnp.bfloat16),
                pltpu.VMEM((max(late), run, width), jnp.bfloat16),
                pltpu.VMEM((n, 2, 2 * rows, width), jnp.float32),
                pltpu.SemaphoreType.DMA((4 * n + 4 * max(late),)),
            ],
        ),
        out_shape=[shape, shape],
        cost_estimate=pl.CostEstimate(
            flops=2 * 3 * 4 * rows * sum(late) * run * width, bytes_accessed=4 * n * (4 * rows * run + 8 * rows * width), transcendentals=0
        ),
        compiler_params=pltpu.CompilerParams(vmem_limit_bytes=VMEM),
        name="finish",
    )(facts, *(array for chunk in begun for array in chunk), bh, bl, sums)


def whole(part, pieces, columns, facts, outs):
    bh, bl, _, sums = columns
    groups, rows, frames = pieces[0].shape
    width, run = bh.shape[1], 2 * frames
    anywhere = pl.BlockSpec(memory_space=SPACE)
    shape = jax.ShapeDtypeStruct((2, 4, rows, width), jnp.float32)
    return pl.pallas_call(
        functools.partial(chunk_kernel, part, 4),
        grid_spec=pltpu.PrefetchScalarGridSpec(
            num_scalar_prefetch=1,
            grid=(),
            in_specs=[anywhere] * 6 + [pl.BlockSpec(memory_space=pltpu.VMEM)] + [anywhere] * 2,
            out_specs=[anywhere, anywhere],
            scratch_shapes=[
                pltpu.VMEM((4, groups, rows, frames), jnp.float32),
                pltpu.VMEM((SLOTS, 2 * rows, frames), jnp.float32),
                pltpu.VMEM((4, run, width), jnp.bfloat16),
                pltpu.VMEM((4, run, width), jnp.bfloat16),
                pltpu.VMEM((4 * rows, width), jnp.float32),
                pltpu.VMEM((2, 2 * rows, width), jnp.float32),
                pltpu.SemaphoreType.DMA((20,)),
            ],
        ),
        out_shape=[shape, shape],
        input_output_aliases={8: 0, 9: 1},
        cost_estimate=pl.CostEstimate(
            flops=2 * 3 * 4 * rows * groups * run * width, bytes_accessed=4 * groups * run * (2 * rows + width), transcendentals=0
        ),
        compiler_params=pltpu.CompilerParams(vmem_limit_bytes=VMEM),
        name="whole",
    )(facts, *pieces, bh, bl, sums, *outs)


def on_device(frames):
    rows, width = frames.shape
    quarter = width // 4
    total = SLOTS * rows
    tm, feat = lax.axis_index("tm"), lax.axis_index("feat")
    y, x_lo, x_hi, z, core = tm // 2, tm % 2, feat // 8, feat // 2 % 4, feat % 2

    quarters = frames.T.reshape(4, quarter, rows)
    spread = [quarters[0]] + [along_z(quarters[n], n) for n in (1, 2, 3)]
    cross = along_x_lo(frames)
    landed = []
    for turn in range(4):
        which = lax.rem(z - pair_in_plane(turn, y) + 4, 4)
        landed.append(to_row_owner(lax.select_n(which, *spread), turn))
    *landed, frames = together(*landed, frames)
    landed = jnp.stack(landed)
    swapped = along_x_hi(landed)
    landed_below, landed_above = along_z(landed, 1), along_z(landed, -1)
    below, above = along_y(frames, 1), along_y(frames, -1)
    swapped, landed_below, landed_above, below, above, cross = together(
        swapped, landed_below, landed_above, below, above, cross
    )

    x_first = x_hi ^ y // 2 ^ y % 2
    runs = [2 * (y % 2 ^ turn // 2) + (x_lo ^ turn % 2) for turn in range(4)]
    times = [2 * run + x for run in runs for x in (x_first, 1 - x_first)]

    def block(away, x_from):
        return lax.rem(y + away + 4, 4) * 2 + x_from

    here, there = x_lo, 1 - x_lo
    order = [block(0, here), block(0, there), block(-1, here), block(1, here)]
    order += [block(-1, there), block(1, there), block(2, here), block(2, there)]
    first = z - (y % 2 * 2 + x_lo)
    chunks = [lax.rem(first + away + 8, 4) for away in (0, -1, 1, 2)]
    facts = jnp.stack([core, *times, *order, *chunks]).astype(jnp.int32)

    swapped_below, swapped_above = along_z(swapped, 1), along_z(swapped, -1)
    cross_below, cross_above = along_y(cross, 1), along_y(cross, -1)
    landed_other, swapped_other = other_core(landed), other_core(swapped)
    columns1 = split_columns([frames, cross, below, above], 0, facts, total)
    begun = [begin(0, 2, (landed, swapped, landed_other, swapped_other), columns1, facts)]
    early_below, early_above, _ = together(landed_below, landed_above, begun[0][1])
    below_other, above_other = other_core(early_below), other_core(early_above)
    swapped_below, swapped_above, cross_below, cross_above, landed_below, below, below_other, above_other = together(
        swapped_below, swapped_above, cross_below, cross_above, landed_below, below, below_other, above_other
    )

    landed_far, swapped_far = along_z(landed_below, 1), along_z(swapped_above, -1)
    far, cross_far = along_y(below, 1), along_y(cross_above, -1)
    columns2 = split_columns([cross_below, cross_above], 4, facts, total, columns1)
    columns3 = split_columns([far, cross_far], 6, facts, total, columns2)
    begun += [
        begin(1, 3, (landed_below, swapped_below, below_other, other_core(swapped_below)), columns2, facts),
        begin(2, 3, (landed_above, swapped_above, above_other, other_core(swapped_above)), columns2, facts),
    ]
    landed_far, swapped_far, _, _ = together(landed_far, swapped_far, begun[1][1], begun[2][1])
    outs = finish(range(3), begun, columns3, facts)
    far_other = other_core(landed_far), other_core(swapped_far)
    outs = whole(3, (landed_far, swapped_far, *far_other), columns3, facts, outs)
    return tuple(out.reshape(2 * width, width) for out in outs)


def solution(mesh):
    return jax.shard_map(
        on_device,
        mesh=mesh,
        in_specs=(P("tm", "feat"),),
        out_specs=(P("tm", "feat"), P("tm", "feat")),
        check_vma=False,
    )
```

```python
import functools

import jax
import jax.numpy as jnp
from jax import lax
from jax.experimental import pallas as pl
from jax.experimental.pallas import tpu as pltpu
from jax.sharding import PartitionSpec as P

LAG = 100
AXES = ("tm", "feat")
DEVICES = 128
SLOTS = 8
VMEM = 24 * 2**20
SPACE = pltpu.HBM
FACTS = {"core": 0, "times": 1, "order": 9, "chunks": 17}


def place(device):
    tm, feat = divmod(device, 16)
    return feat // 8, tm % 2, tm // 2, feat // 2 % 4, feat % 2


def device_at(x_hi, x_lo, y, z, core):
    return (y % 4 * 2 + x_lo) * 16 + (x_hi * 4 + z % 4) * 2 + core


def move(block, step):
    route = [(d, device_at(*step(*place(d)))) for d in range(DEVICES)]
    return lax.ppermute(block, AXES, route)


def along_x_lo(block):
    return move(block, lambda xh, xl, y, z, c: (xh, 1 - xl, y, z, c))


def along_x_hi(block):
    return move(block, lambda xh, xl, y, z, c: (1 - xh, xl, y, z, c))


def along_y(block, n):
    return move(block, lambda xh, xl, y, z, c: (xh, xl, y + n, z, c))


def along_z(block, n):
    return move(block, lambda xh, xl, y, z, c: (xh, xl, y, z + n, c))


def other_core(block):
    return move(block, lambda xh, xl, y, z, c: (xh, xl, y, z, 1 - c))


def together(*blocks):
    return lax.optimization_barrier(blocks)


def pair_in_plane(turn, y):
    return 2 * (turn // 2 ^ y // 2) + (turn % 2 ^ y % 2)


def to_row_owner(block, turn):
    def step(xh, xl, y, z, c):
        pair = pair_in_plane(turn, y)
        return xh ^ pair // 2 ^ xl, pair % 2, 2 * xh + pair // 2, z, c

    return move(block, step)


def split(x):
    high = x.astype(jnp.bfloat16)
    return high, (x - high.astype(jnp.float32)).astype(jnp.bfloat16)


def columns_kernel(sizes, skip, first, facts_ref, *refs):
    n = len(sizes)
    pieces, refs = refs[:n], refs[n:]
    if first:
        high_out, low_out, centre_out, sums_out, high, low, sems = refs
    else:
        centre_in, sums_in, _, _, high_out, low_out, sums_out, high, low, sems = refs
    size = sizes[0]
    copies = []
    for i in range(n):
        block = pieces[i][...]
        if first and i == 0:
            centre = jnp.sum(block, axis=0, keepdims=True) / size
            centre_out[...] = centre
            sums = jnp.zeros_like(centre)
        elif i == 0:
            centre, sums = centre_in[...], sums_in[...]
        block = block - centre
        sums = sums + jnp.sum(block, axis=0, keepdims=True)
        high[i], low[i] = split(block)
        there = pl.ds(pl.multiple_of(facts_ref[FACTS["order"] + skip + i] * size, size), size)
        for j, (held, out) in enumerate(((high, high_out), (low, low_out))):
            copy = pltpu.make_async_copy(held.at[i], out.at[there], sems.at[2 * i + j])
            copy.start()
            copies.append(copy)
    sums_out[...] = sums
    for copy in copies:
        copy.wait()


def split_columns(pieces, skip, facts, total, state=None):
    sizes = [p.shape[0] for p in pieces]
    width = pieces[0].shape[1]
    n, first = len(pieces), state is None
    whole = jax.ShapeDtypeStruct((total, width), jnp.bfloat16)
    line = jax.ShapeDtypeStruct((1, width), jnp.float32)
    anywhere = pl.BlockSpec(memory_space=SPACE)
    held = pl.BlockSpec(memory_space=pltpu.VMEM)
    more, more_specs, aliases = [], [], {}
    if not first:
        high, low, centre, sums = state
        more, more_specs = [centre, sums, high, low], [held, held, anywhere, anywhere]
        aliases = {n + 3: 0, n + 4: 1}
    count = sum(sizes) * width
    out = pl.pallas_call(
        functools.partial(columns_kernel, sizes, skip, first),
        grid_spec=pltpu.PrefetchScalarGridSpec(
            num_scalar_prefetch=1,
            grid=(),
            in_specs=[held] * n + more_specs,
            out_specs=[anywhere, anywhere] + [held] * (2 if first else 1),
            scratch_shapes=[
                pltpu.VMEM((n, sizes[0], width), jnp.bfloat16),
                pltpu.VMEM((n, sizes[0], width), jnp.bfloat16),
                pltpu.SemaphoreType.DMA((2 * n,)),
            ],
        ),
        out_shape=[whole, whole] + [line] * (2 if first else 1),
        input_output_aliases=aliases,
        cost_estimate=pl.CostEstimate(flops=count, bytes_accessed=2 * count, transcendentals=0),
        compiler_params=pltpu.CompilerParams(vmem_limit_bytes=VMEM),
        name="split_columns",
    )(facts, *pieces, *more)
    if first:
        return out
    return out[0], out[1], state[2], out[2]


def start_columns(facts_ref, pairs, sources, held, sems, newest_first=False):
    copies = []
    size = held[0].shape[1] // 2
    for n, pair in enumerate(pairs):
        for i in range(2):
            row = facts_ref[FACTS["order"] + 2 * pair + i] * size
            for j in range(2):
                copies.append(
                    pltpu.make_async_copy(
                        sources[j].at[pl.ds(pl.multiple_of(row, size), size)],
                        held[j].at[n, pl.ds(i * size, size)],
                        sems.at[4 * n + 2 * i + j],
                    )
                )
    for n in range(len(pairs)) if not newest_first else reversed(range(len(pairs))):
        for copy in copies[4 * n : 4 * n + 4]:
            copy.start()
    return copies


def write_out(facts_ref, total, edge, sums, count, outs, done, parts, sems):
    rows = total.shape[0] // 4
    done[0] = total[: 2 * rows] / count
    done[1] = (total[2 * rows :] - edge * (sums / count)) / (count - LAG)
    copies = []
    for i, out in enumerate(outs):
        for half in range(2):
            there = out.at[half, facts_ref[FACTS["chunks"] + parts]]
            here = done.at[i, pl.ds(half * rows, rows)]
            copies.append(pltpu.make_async_copy(here, there, sems.at[2 * i + half]))
            copies[-1].start()
    return copies


dot = functools.partial(jnp.dot, preferred_element_type=jnp.float32)


def chunk_kernel(part, ready, facts_ref, *refs):
    last = ready == 4
    pieces, (bh_in, bl_in), refs = refs[:4], refs[4:6], refs[6:]
    if last:
        sums, _, _, instant_out, lagged_out, held, bh, bl, total, done, sems = refs
    else:
        total, edge_out, high_out, low_out, held, bh, bl, sems = refs
    groups, rows, frames = pieces[0].shape

    b_copies = start_columns(facts_ref, range(ready), (bh_in, bl_in), (bh, bl), sems.at[pl.ds(4, 16)])

    for half in range(2):
        sum_ = jnp.zeros((rows, frames), jnp.float32)
        for g in range(groups):
            sum_ = sum_ + (pieces[2 * half][g] + pieces[2 * half + 1][g])
        mean = jnp.sum(sum_, axis=1, keepdims=True) / (2 * groups * frames)
        core = facts_ref[FACTS["core"]]
        core = core if half == 0 else 1 - core
        there = pl.ds(pl.multiple_of(core * rows, rows), rows)
        for i in range(2):
            for g in range(groups):
                held[facts_ref[FACTS["times"] + 2 * g + i], there, :] = pieces[2 * half + i][g] - mean

    edge = jnp.zeros((2 * rows, 1), jnp.float32)
    lane = lax.broadcasted_iota(jnp.int32, (2 * rows, frames), 1)
    for pair in range(4):
        now, shifted = [], []
        for i in range(2):
            time = facts_ref[FACTS["order"] + 2 * pair + i]
            now.append(held[time])
            before = held[jnp.maximum(time - 1, 0)]
            before = jnp.where(time == 0, 0.0, before)
            moved = jnp.where(lane < LAG, pltpu.roll(before, LAG, 1), pltpu.roll(now[i], LAG, 1))
            edge = edge + jnp.sum(moved, axis=1, keepdims=True)
            shifted.append(moved)
        both = [jnp.concatenate(blocks, axis=1) for blocks in (now, shifted)]
        high, low = split(jnp.concatenate(both, axis=0))
        if pair >= ready:
            high_out[pair - ready], low_out[pair - ready] = high, low
            continue
        for copy in b_copies[4 * pair : 4 * pair + 4]:
            copy.wait()
        product = dot(high, bh[pair]) + dot(low, bh[pair]) + dot(high, bl[pair])
        if pair == 0:
            total[...] = product
        else:
            total[...] += product
    if last:
        copies = write_out(
            facts_ref, total, edge, sums[...], 2 * groups * frames, (instant_out, lagged_out), done, part, sems
        )
        for copy in copies:
            copy.wait()
    else:
        edge_out[...] = jnp.broadcast_to(edge, edge_out.shape)


def finish_kernel(parts, facts_ref, *refs):
    n = len(parts)
    begun, (bh_in, bl_in, sums, instant_out, lagged_out), refs = refs[: 4 * n], refs[4 * n : 4 * n + 5], refs[4 * n + 5 :]
    bh, bl, done, sems = refs
    late = [begun[4 * i + 2].shape[0] for i in range(n)]
    pairs = range(4 - max(late), 4)
    here = sems.at[pl.ds(4 * n, 4 * len(pairs))]
    b_copies = start_columns(facts_ref, pairs, (bh_in, bl_in), (bh, bl), here, True)
    copies, waited = [], len(pairs)
    for i in sorted(range(n), key=lambda i: late[i]):
        part = parts[i]
        for copy in b_copies[4 * (len(pairs) - late[i]) : 4 * waited]:
            copy.wait()
        waited = min(waited, len(pairs) - late[i])
        total, edge, high, low = begun[4 * i : 4 * i + 4]
        now = total[...]
        for j in range(late[i]):
            k = j + max(late) - late[i]
            now = now + (dot(high[j], bh[k]) + dot(low[j], bh[k]) + dot(high[j], bl[k]))
        count = 4 * high.shape[2]
        copies += write_out(
            facts_ref, now, edge[:, :1], sums[...], count, (instant_out, lagged_out), done.at[i], part, sems.at[pl.ds(4 * i, 4)]
        )
    for copy in copies:
        copy.wait()


def begin(part, ready, pieces, columns, facts):
    bh, bl = columns[:2]
    groups, rows, frames = pieces[0].shape
    width, run = bh.shape[1], 2 * frames
    anywhere = pl.BlockSpec(memory_space=SPACE)
    held = pl.BlockSpec(memory_space=pltpu.VMEM)
    return pl.pallas_call(
        functools.partial(chunk_kernel, part, ready),
        grid_spec=pltpu.PrefetchScalarGridSpec(
            num_scalar_prefetch=1,
            grid=(),
            in_specs=[held] * 4 + [anywhere] * 2,
            out_specs=[held] * 4,
            scratch_shapes=[
                pltpu.VMEM((SLOTS, 2 * rows, frames), jnp.float32),
                pltpu.VMEM((ready, run, width), jnp.bfloat16),
                pltpu.VMEM((ready, run, width), jnp.bfloat16),
                pltpu.SemaphoreType.DMA((20,)),
            ],
        ),
        out_shape=[
            jax.ShapeDtypeStruct((4 * rows, width), jnp.float32),
            jax.ShapeDtypeStruct((2 * rows, 128), jnp.float32),
            jax.ShapeDtypeStruct((4 - ready, 4 * rows, run), jnp.bfloat16),
            jax.ShapeDtypeStruct((4 - ready, 4 * rows, run), jnp.bfloat16),
        ],
        cost_estimate=pl.CostEstimate(
            flops=rows * ready * run * width, bytes_accessed=groups * run * (2 * rows + width), transcendentals=0
        ),
        compiler_params=pltpu.CompilerParams(vmem_limit_bytes=VMEM),
        name="begin",
    )(facts, *pieces, bh, bl)


def finish(parts, begun, columns, facts):
    bh, bl, _, sums = columns
    rows, width = begun[0][1].shape[0] // 2, bh.shape[1]
    run = begun[0][2].shape[2]
    late = [chunk[2].shape[0] for chunk in begun]
    anywhere = pl.BlockSpec(memory_space=SPACE)
    held = pl.BlockSpec(memory_space=pltpu.VMEM)
    shape = jax.ShapeDtypeStruct((2, 4, rows, width), jnp.float32)
    n = len(parts)
    return pl.pallas_call(
        functools.partial(finish_kernel, parts),
        grid_spec=pltpu.PrefetchScalarGridSpec(
            num_scalar_prefetch=1,
            grid=(),
            in_specs=[held] * (4 * n) + [anywhere] * 2 + [held],
            out_specs=[anywhere, anywhere],
            scratch_shapes=[
                pltpu.VMEM((max(late), run, width), jnp.bfloat16),
                pltpu.VMEM((max(late), run, width), jnp.bfloat16),
                pltpu.VMEM((n, 2, 2 * rows, width), jnp.float32),
                pltpu.SemaphoreType.DMA((4 * n + 4 * max(late),)),
            ],
        ),
        out_shape=[shape, shape],
        cost_estimate=pl.CostEstimate(
            flops=2 * 3 * 4 * rows * sum(late) * run * width, bytes_accessed=4 * n * (4 * rows * run + 8 * rows * width), transcendentals=0
        ),
        compiler_params=pltpu.CompilerParams(vmem_limit_bytes=VMEM),
        name="finish",
    )(facts, *(array for chunk in begun for array in chunk), bh, bl, sums)


def whole(part, pieces, columns, facts, outs):
    bh, bl, _, sums = columns
    groups, rows, frames = pieces[0].shape
    width, run = bh.shape[1], 2 * frames
    anywhere = pl.BlockSpec(memory_space=SPACE)
    held = pl.BlockSpec(memory_space=pltpu.VMEM)
    shape = jax.ShapeDtypeStruct((2, 4, rows, width), jnp.float32)
    return pl.pallas_call(
        functools.partial(chunk_kernel, part, 4),
        grid_spec=pltpu.PrefetchScalarGridSpec(
            num_scalar_prefetch=1,
            grid=(),
            in_specs=[held] * 4 + [anywhere] * 2 + [held] + [anywhere] * 2,
            out_specs=[anywhere, anywhere],
            scratch_shapes=[
                pltpu.VMEM((SLOTS, 2 * rows, frames), jnp.float32),
                pltpu.VMEM((4, run, width), jnp.bfloat16),
                pltpu.VMEM((4, run, width), jnp.bfloat16),
                pltpu.VMEM((4 * rows, width), jnp.float32),
                pltpu.VMEM((2, 2 * rows, width), jnp.float32),
                pltpu.SemaphoreType.DMA((20,)),
            ],
        ),
        out_shape=[shape, shape],
        input_output_aliases={8: 0, 9: 1},
        cost_estimate=pl.CostEstimate(
            flops=2 * 3 * 4 * rows * groups * run * width, bytes_accessed=4 * groups * run * (2 * rows + width), transcendentals=0
        ),
        compiler_params=pltpu.CompilerParams(vmem_limit_bytes=VMEM),
        name="whole",
    )(facts, *pieces, bh, bl, sums, *outs)


def on_device(frames):
    rows, width = frames.shape
    quarter = width // 4
    total = SLOTS * rows
    tm, feat = lax.axis_index("tm"), lax.axis_index("feat")
    y, x_lo, x_hi, z, core = tm // 2, tm % 2, feat // 8, feat // 2 % 4, feat % 2

    quarters = frames.T.reshape(4, quarter, rows)
    spread = [quarters[0]] + [along_z(quarters[n], n) for n in (1, 2, 3)]
    cross = along_x_lo(frames)
    landed = []
    for turn in range(4):
        which = lax.rem(z - pair_in_plane(turn, y) + 4, 4)
        piece = lax.select_n(which, *spread)
        if turn in (0, 1):
            piece, cross = together(piece, cross)
        landed.append(to_row_owner(piece, turn))
    *landed, frames = together(*landed, frames)
    landed = jnp.stack(landed)
    swapped = along_x_hi(landed)
    landed_below, landed_above = along_z(landed, 1), along_z(landed, -1)
    below, above = along_y(frames, 1), along_y(frames, -1)
    landed_other = other_core(landed)
    swapped, landed_below, landed_above, below, above, cross, landed_other = together(
        swapped, landed_below, landed_above, below, above, cross, landed_other
    )

    x_first = x_hi ^ y // 2 ^ y % 2
    runs = [2 * (y % 2 ^ turn // 2) + (x_lo ^ turn % 2) for turn in range(4)]
    times = [2 * run + x for run in runs for x in (x_first, 1 - x_first)]

    def block(away, x_from):
        return lax.rem(y + away + 4, 4) * 2 + x_from

    here, there = x_lo, 1 - x_lo
    order = [block(0, here), block(0, there), block(-1, here), block(1, here)]
    order += [block(-1, there), block(1, there), block(2, here), block(2, there)]
    first = z - (y % 2 * 2 + x_lo)
    chunks = [lax.rem(first + away + 8, 4) for away in (0, -1, 1, 2)]
    facts = jnp.stack([core, *times, *order, *chunks]).astype(jnp.int32)

    swapped_below, swapped_above = along_z(swapped, 1), along_z(swapped, -1)
    cross_below, cross_above = along_y(cross, 1), along_y(cross, -1)
    swapped_other = other_core(swapped)
    columns1 = split_columns([frames, cross, below, above], 0, facts, total)
    begun = [begin(0, 2, (landed, swapped, landed_other, swapped_other), columns1, facts)]
    early_below, early_above, _ = together(landed_below, landed_above, begun[0][1])
    below_other, above_other = other_core(early_below), other_core(early_above)
    swapped_below, swapped_above, cross_below, cross_above, landed_below, below, below_other, above_other = together(
        swapped_below, swapped_above, cross_below, cross_above, landed_below, below, below_other, above_other
    )

    landed_far, swapped_far = along_z(landed_below, 1), along_z(swapped_above, -1)
    far, cross_far = along_y(below, 1), along_y(cross_above, -1)
    columns2 = split_columns([cross_below, cross_above], 4, facts, total, columns1)
    columns3 = split_columns([far, cross_far], 6, facts, total, columns2)
    begun.append(begin(1, 3, (landed_below, swapped_below, below_other, other_core(swapped_below)), columns2, facts))
    begun.append(begin(2, 3, (landed_above, swapped_above, above_other, other_core(swapped_above)), columns2, facts))
    landed_far, swapped_far, _, _ = together(landed_far, swapped_far, begun[1][1], begun[2][1])
    outs = finish(range(3), begun, columns3, facts)
    far_other = other_core(landed_far), other_core(swapped_far)
    outs = whole(3, (landed_far, swapped_far, *far_other), columns3, facts, outs)
    return tuple(out.reshape(2 * width, width) for out in outs)


def solution(mesh):
    return jax.shard_map(
        on_device,
        mesh=mesh,
        in_specs=(P("tm", "feat"),),
        out_specs=(P("tm", "feat"), P("tm", "feat")),
        check_vma=False,
    )
```

```python
import functools

import jax
import jax.numpy as jnp
from jax import lax
from jax.experimental import pallas as pl
from jax.experimental.pallas import tpu as pltpu
from jax.sharding import PartitionSpec as P

LAG = 100
AXES = ("tm", "feat")
DEVICES = 128
SLOTS = 8
VMEM = 24 * 2**20
SPACE = pltpu.HBM
FACTS = {"core": 0, "times": 1, "order": 9, "chunks": 17}


def place(device):
    tm, feat = divmod(device, 16)
    return feat // 8, tm % 2, tm // 2, feat // 2 % 4, feat % 2


def device_at(x_hi, x_lo, y, z, core):
    return (y % 4 * 2 + x_lo) * 16 + (x_hi * 4 + z % 4) * 2 + core


def move(block, step):
    route = [(d, device_at(*step(*place(d)))) for d in range(DEVICES)]
    return lax.ppermute(block, AXES, route)


def along_x_lo(block):
    return move(block, lambda xh, xl, y, z, c: (xh, 1 - xl, y, z, c))


def along_x_hi(block):
    return move(block, lambda xh, xl, y, z, c: (1 - xh, xl, y, z, c))


def along_y(block, n):
    return move(block, lambda xh, xl, y, z, c: (xh, xl, y + n, z, c))


def along_z(block, n):
    return move(block, lambda xh, xl, y, z, c: (xh, xl, y, z + n, c))


def other_core(block):
    return move(block, lambda xh, xl, y, z, c: (xh, xl, y, z, 1 - c))


def together(*blocks):
    return lax.optimization_barrier(blocks)


def pair_in_plane(turn, y):
    return 2 * (turn // 2 ^ y // 2) + (turn % 2 ^ y % 2)


def to_row_owner(block, turn):
    def step(xh, xl, y, z, c):
        pair = pair_in_plane(turn, y)
        return xh ^ pair % 2 ^ xl, pair % 2, 2 * xh + pair // 2, z, c

    return move(block, step)


def split(x):
    high = x.astype(jnp.bfloat16)
    return high, (x - high.astype(jnp.float32)).astype(jnp.bfloat16)


def columns_kernel(sizes, skip, first, facts_ref, *refs):
    n = len(sizes)
    pieces, refs = refs[:n], refs[n:]
    if first:
        high_out, low_out, centre_out, sums_out, high, low, sems = refs
    else:
        centre_in, sums_in, _, _, high_out, low_out, sums_out, high, low, sems = refs
    size = sizes[0]
    copies = []
    for i in range(n):
        block = pieces[i][...]
        if first and i == 0:
            centre = jnp.sum(block, axis=0, keepdims=True) / size
            centre_out[...] = centre
            sums = jnp.zeros_like(centre)
        elif i == 0:
            centre, sums = centre_in[...], sums_in[...]
        block = block - centre
        sums = sums + jnp.sum(block, axis=0, keepdims=True)
        high[i], low[i] = split(block)
        there = pl.ds(pl.multiple_of(facts_ref[FACTS["order"] + skip + i] * size, size), size)
        for j, (held, out) in enumerate(((high, high_out), (low, low_out))):
            copy = pltpu.make_async_copy(held.at[i], out.at[there], sems.at[2 * i + j])
            copy.start()
            copies.append(copy)
    sums_out[...] = sums
    for copy in copies:
        copy.wait()


def split_columns(pieces, skip, facts, total, state=None):
    sizes = [p.shape[0] for p in pieces]
    width = pieces[0].shape[1]
    n, first = len(pieces), state is None
    whole = jax.ShapeDtypeStruct((total, width), jnp.bfloat16)
    line = jax.ShapeDtypeStruct((1, width), jnp.float32)
    anywhere = pl.BlockSpec(memory_space=SPACE)
    held = pl.BlockSpec(memory_space=pltpu.VMEM)
    more, more_specs, aliases = [], [], {}
    if not first:
        high, low, centre, sums = state
        more, more_specs = [centre, sums, high, low], [held, held, anywhere, anywhere]
        aliases = {n + 3: 0, n + 4: 1}
    count = sum(sizes) * width
    out = pl.pallas_call(
        functools.partial(columns_kernel, sizes, skip, first),
        grid_spec=pltpu.PrefetchScalarGridSpec(
            num_scalar_prefetch=1,
            grid=(),
            in_specs=[held] * n + more_specs,
            out_specs=[anywhere, anywhere] + [held] * (2 if first else 1),
            scratch_shapes=[
                pltpu.VMEM((n, sizes[0], width), jnp.bfloat16),
                pltpu.VMEM((n, sizes[0], width), jnp.bfloat16),
                pltpu.SemaphoreType.DMA((2 * n,)),
            ],
        ),
        out_shape=[whole, whole] + [line] * (2 if first else 1),
        input_output_aliases=aliases,
        cost_estimate=pl.CostEstimate(flops=count, bytes_accessed=2 * count, transcendentals=0),
        compiler_params=pltpu.CompilerParams(vmem_limit_bytes=VMEM),
        name="split_columns",
    )(facts, *pieces, *more)
    if first:
        return out
    return out[0], out[1], state[2], out[2]


def start_columns(facts_ref, pairs, sources, held, sems, newest_first=False):
    copies = []
    size = held[0].shape[1] // 2
    for n, pair in enumerate(pairs):
        for i in range(2):
            row = facts_ref[FACTS["order"] + 2 * pair + i] * size
            for j in range(2):
                copies.append(
                    pltpu.make_async_copy(
                        sources[j].at[pl.ds(pl.multiple_of(row, size), size)],
                        held[j].at[n, pl.ds(i * size, size)],
                        sems.at[4 * n + 2 * i + j],
                    )
                )
    for n in range(len(pairs)) if not newest_first else reversed(range(len(pairs))):
        for copy in copies[4 * n : 4 * n + 4]:
            copy.start()
    return copies


def write_out(facts_ref, total, edge, sums, count, outs, done, parts, sems):
    rows = total.shape[0] // 4
    done[0] = total[: 2 * rows] / count
    done[1] = (total[2 * rows :] - edge * (sums / count)) / (count - LAG)
    copies = []
    for i, out in enumerate(outs):
        for half in range(2):
            there = out.at[half, facts_ref[FACTS["chunks"] + parts]]
            here = done.at[i, pl.ds(half * rows, rows)]
            copies.append(pltpu.make_async_copy(here, there, sems.at[2 * i + half]))
            copies[-1].start()
    return copies


dot = functools.partial(jnp.dot, preferred_element_type=jnp.float32)


def chunk_kernel(part, ready, facts_ref, *refs):
    last = ready == 4
    pieces, (bh_in, bl_in), refs = refs[:4], refs[4:6], refs[6:]
    if last:
        sums, _, _, instant_out, lagged_out, held, bh, bl, total, done, sems = refs
    else:
        total, edge_out, high_out, low_out, held, bh, bl, sems = refs
    groups, rows, frames = pieces[0].shape

    b_copies = start_columns(facts_ref, range(ready), (bh_in, bl_in), (bh, bl), sems.at[pl.ds(4, 16)])

    for half in range(2):
        sum_ = jnp.zeros((rows, frames), jnp.float32)
        for g in range(groups):
            sum_ = sum_ + (pieces[2 * half][g] + pieces[2 * half + 1][g])
        mean = jnp.sum(sum_, axis=1, keepdims=True) / (2 * groups * frames)
        core = facts_ref[FACTS["core"]]
        core = core if half == 0 else 1 - core
        there = pl.ds(pl.multiple_of(core * rows, rows), rows)
        for i in range(2):
            for g in range(groups):
                held[facts_ref[FACTS["times"] + 2 * g + i], there, :] = pieces[2 * half + i][g] - mean

    edge = jnp.zeros((2 * rows, 1), jnp.float32)
    lane = lax.broadcasted_iota(jnp.int32, (2 * rows, frames), 1)
    for pair in range(4):
        now, shifted = [], []
        for i in range(2):
            time = facts_ref[FACTS["order"] + 2 * pair + i]
            now.append(held[time])
            before = held[jnp.maximum(time - 1, 0)]
            before = jnp.where(time == 0, 0.0, before)
            moved = jnp.where(lane < LAG, pltpu.roll(before, LAG, 1), pltpu.roll(now[i], LAG, 1))
            edge = edge + jnp.sum(moved, axis=1, keepdims=True)
            shifted.append(moved)
        both = [jnp.concatenate(blocks, axis=1) for blocks in (now, shifted)]
        high, low = split(jnp.concatenate(both, axis=0))
        if pair >= ready:
            high_out[pair - ready], low_out[pair - ready] = high, low
            continue
        for copy in b_copies[4 * pair : 4 * pair + 4]:
            copy.wait()
        product = dot(high, bh[pair]) + dot(low, bh[pair]) + dot(high, bl[pair])
        if pair == 0:
            total[...] = product
        else:
            total[...] += product
    if last:
        copies = write_out(
            facts_ref, total, edge, sums[...], 2 * groups * frames, (instant_out, lagged_out), done, part, sems
        )
        for copy in copies:
            copy.wait()
    else:
        edge_out[...] = jnp.broadcast_to(edge, edge_out.shape)


def finish_kernel(parts, facts_ref, *refs):
    n = len(parts)
    begun, (bh_in, bl_in, sums, instant_out, lagged_out), refs = refs[: 4 * n], refs[4 * n : 4 * n + 5], refs[4 * n + 5 :]
    bh, bl, done, sems = refs
    late = [begun[4 * i + 2].shape[0] for i in range(n)]
    pairs = range(4 - max(late), 4)
    here = sems.at[pl.ds(4 * n, 4 * len(pairs))]
    b_copies = start_columns(facts_ref, pairs, (bh_in, bl_in), (bh, bl), here, True)
    copies, waited = [], len(pairs)
    for i in sorted(range(n), key=lambda i: late[i]):
        part = parts[i]
        for copy in b_copies[4 * (len(pairs) - late[i]) : 4 * waited]:
            copy.wait()
        waited = min(waited, len(pairs) - late[i])
        total, edge, high, low = begun[4 * i : 4 * i + 4]
        now = total[...]
        for j in range(late[i]):
            k = j + max(late) - late[i]
            now = now + (dot(high[j], bh[k]) + dot(low[j], bh[k]) + dot(high[j], bl[k]))
        count = 4 * high.shape[2]
        copies += write_out(
            facts_ref, now, edge[:, :1], sums[...], count, (instant_out, lagged_out), done.at[i], part, sems.at[pl.ds(4 * i, 4)]
        )
    for copy in copies:
        copy.wait()


def begin(part, ready, pieces, columns, facts):
    bh, bl = columns[:2]
    groups, rows, frames = pieces[0].shape
    width, run = bh.shape[1], 2 * frames
    anywhere = pl.BlockSpec(memory_space=SPACE)
    held = pl.BlockSpec(memory_space=pltpu.VMEM)
    return pl.pallas_call(
        functools.partial(chunk_kernel, part, ready),
        grid_spec=pltpu.PrefetchScalarGridSpec(
            num_scalar_prefetch=1,
            grid=(),
            in_specs=[held] * 4 + [anywhere] * 2,
            out_specs=[held] * 4,
            scratch_shapes=[
                pltpu.VMEM((SLOTS, 2 * rows, frames), jnp.float32),
                pltpu.VMEM((ready, run, width), jnp.bfloat16),
                pltpu.VMEM((ready, run, width), jnp.bfloat16),
                pltpu.SemaphoreType.DMA((20,)),
            ],
        ),
        out_shape=[
            jax.ShapeDtypeStruct((4 * rows, width), jnp.float32),
            jax.ShapeDtypeStruct((2 * rows, 128), jnp.float32),
            jax.ShapeDtypeStruct((4 - ready, 4 * rows, run), jnp.bfloat16),
            jax.ShapeDtypeStruct((4 - ready, 4 * rows, run), jnp.bfloat16),
        ],
        cost_estimate=pl.CostEstimate(
            flops=rows * ready * run * width, bytes_accessed=groups * run * (2 * rows + width), transcendentals=0
        ),
        compiler_params=pltpu.CompilerParams(vmem_limit_bytes=VMEM),
        name="begin",
    )(facts, *pieces, bh, bl)


def finish(parts, begun, columns, facts):
    bh, bl, _, sums = columns
    rows, width = begun[0][1].shape[0] // 2, bh.shape[1]
    run = begun[0][2].shape[2]
    late = [chunk[2].shape[0] for chunk in begun]
    anywhere = pl.BlockSpec(memory_space=SPACE)
    held = pl.BlockSpec(memory_space=pltpu.VMEM)
    shape = jax.ShapeDtypeStruct((2, 4, rows, width), jnp.float32)
    n = len(parts)
    return pl.pallas_call(
        functools.partial(finish_kernel, parts),
        grid_spec=pltpu.PrefetchScalarGridSpec(
            num_scalar_prefetch=1,
            grid=(),
            in_specs=[held] * (4 * n) + [anywhere] * 2 + [held],
            out_specs=[anywhere, anywhere],
            scratch_shapes=[
                pltpu.VMEM((max(late), run, width), jnp.bfloat16),
                pltpu.VMEM((max(late), run, width), jnp.bfloat16),
                pltpu.VMEM((n, 2, 2 * rows, width), jnp.float32),
                pltpu.SemaphoreType.DMA((4 * n + 4 * max(late),)),
            ],
        ),
        out_shape=[shape, shape],
        cost_estimate=pl.CostEstimate(
            flops=2 * 3 * 4 * rows * sum(late) * run * width, bytes_accessed=4 * n * (4 * rows * run + 8 * rows * width), transcendentals=0
        ),
        compiler_params=pltpu.CompilerParams(vmem_limit_bytes=VMEM),
        name="finish",
    )(facts, *(array for chunk in begun for array in chunk), bh, bl, sums)


def whole(part, pieces, columns, facts, outs):
    bh, bl, _, sums = columns
    groups, rows, frames = pieces[0].shape
    width, run = bh.shape[1], 2 * frames
    anywhere = pl.BlockSpec(memory_space=SPACE)
    held = pl.BlockSpec(memory_space=pltpu.VMEM)
    shape = jax.ShapeDtypeStruct((2, 4, rows, width), jnp.float32)
    return pl.pallas_call(
        functools.partial(chunk_kernel, part, 4),
        grid_spec=pltpu.PrefetchScalarGridSpec(
            num_scalar_prefetch=1,
            grid=(),
            in_specs=[held] * 4 + [anywhere] * 2 + [held] + [anywhere] * 2,
            out_specs=[anywhere, anywhere],
            scratch_shapes=[
                pltpu.VMEM((SLOTS, 2 * rows, frames), jnp.float32),
                pltpu.VMEM((4, run, width), jnp.bfloat16),
                pltpu.VMEM((4, run, width), jnp.bfloat16),
                pltpu.VMEM((4 * rows, width), jnp.float32),
                pltpu.VMEM((2, 2 * rows, width), jnp.float32),
                pltpu.SemaphoreType.DMA((20,)),
            ],
        ),
        out_shape=[shape, shape],
        input_output_aliases={8: 0, 9: 1},
        cost_estimate=pl.CostEstimate(
            flops=2 * 3 * 4 * rows * groups * run * width, bytes_accessed=4 * groups * run * (2 * rows + width), transcendentals=0
        ),
        compiler_params=pltpu.CompilerParams(vmem_limit_bytes=VMEM),
        name="whole",
    )(facts, *pieces, bh, bl, sums, *outs)


def on_device(frames):
    rows, width = frames.shape
    quarter = width // 4
    total = SLOTS * rows
    tm, feat = lax.axis_index("tm"), lax.axis_index("feat")
    y, x_lo, x_hi, z, core = tm // 2, tm % 2, feat // 8, feat // 2 % 4, feat % 2

    quarters = frames.T.reshape(4, quarter, rows)
    spread = [quarters[0]] + [along_z(quarters[n], n) for n in (1, 2, 3)]
    cross = along_x_lo(frames)
    landed = []
    for turn in range(4):
        which = lax.rem(z - pair_in_plane(turn, y) + 4, 4)
        piece = lax.select_n(which, *spread)
        if turn in (0, 1):
            piece, cross = together(piece, cross)
        landed.append(to_row_owner(piece, turn))
    *landed, frames = together(*landed, frames)
    landed = jnp.stack(landed)
    swapped = along_x_hi(landed)
    landed_below, landed_above = along_z(landed, 1), along_z(landed, -1)
    below, above = along_y(frames, 1), along_y(frames, -1)
    landed_other = other_core(landed)
    swapped, landed_below, landed_above, below, above, cross, landed_other = together(
        swapped, landed_below, landed_above, below, above, cross, landed_other
    )

    x_first = x_hi ^ y // 2 ^ x_lo
    runs = [2 * (y % 2 ^ turn // 2) + (x_lo ^ turn % 2) for turn in range(4)]
    times = [2 * run + x for run in runs for x in (x_first, 1 - x_first)]

    def block(away, x_from):
        return lax.rem(y + away + 4, 4) * 2 + x_from

    here, there = x_lo, 1 - x_lo
    order = [block(0, here), block(0, there), block(-1, here), block(1, here)]
    order += [block(-1, there), block(1, there), block(2, here), block(2, there)]
    first = z - (y % 2 * 2 + x_lo)
    chunks = [lax.rem(first + away + 8, 4) for away in (0, -1, 1, 2)]
    facts = jnp.stack([core, *times, *order, *chunks]).astype(jnp.int32)

    swapped_below, swapped_above = along_z(swapped, 1), along_z(swapped, -1)
    cross_below, cross_above = along_y(cross, 1), along_y(cross, -1)
    swapped_other = other_core(swapped)
    columns1 = split_columns([frames, cross, below, above], 0, facts, total)
    begun = [begin(0, 2, (landed, swapped, landed_other, swapped_other), columns1, facts)]
    early_below, early_above, _ = together(landed_below, landed_above, begun[0][1])
    below_other, above_other = other_core(early_below), other_core(early_above)
    swapped_below, swapped_above, cross_below, cross_above, landed_below, below, below_other, above_other = together(
        swapped_below, swapped_above, cross_below, cross_above, landed_below, below, below_other, above_other
    )

    landed_far, swapped_far = along_z(landed_below, 1), along_z(swapped_above, -1)
    far, cross_far = along_y(below, 1), along_y(cross_above, -1)
    columns2 = split_columns([cross_below, cross_above], 4, facts, total, columns1)
    columns3 = split_columns([far, cross_far], 6, facts, total, columns2)
    begun.append(begin(1, 3, (landed_below, swapped_below, below_other, other_core(swapped_below)), columns2, facts))
    begun.append(begin(2, 3, (landed_above, swapped_above, above_other, other_core(swapped_above)), columns2, facts))
    landed_far, swapped_far, _, _ = together(landed_far, swapped_far, begun[1][1], begun[2][1])
    outs = finish(range(3), begun, columns3, facts)
    far_other = other_core(landed_far), other_core(swapped_far)
    outs = whole(3, (landed_far, swapped_far, *far_other), columns3, facts, outs)
    return tuple(out.reshape(2 * width, width) for out in outs)


def solution(mesh):
    return jax.shard_map(
        on_device,
        mesh=mesh,
        in_specs=(P("tm", "feat"),),
        out_specs=(P("tm", "feat"), P("tm", "feat")),
        check_vma=False,
    )
```

```python
import functools

import jax
import jax.numpy as jnp
from jax import lax
from jax.experimental import pallas as pl
from jax.experimental.pallas import tpu as pltpu
from jax.sharding import PartitionSpec as P

LAG = 100
AXES = ("tm", "feat")
DEVICES = 128
SLOTS = 8
VMEM = 24 * 2**20
SPACE = pltpu.HBM
FACTS = {"core": 0, "times": 1, "order": 9, "chunks": 17}


def place(device):
    tm, feat = divmod(device, 16)
    return feat // 8, tm % 2, tm // 2, feat // 2 % 4, feat % 2


def device_at(x_hi, x_lo, y, z, core):
    return (y % 4 * 2 + x_lo) * 16 + (x_hi * 4 + z % 4) * 2 + core


def move(block, step):
    route = [(d, device_at(*step(*place(d)))) for d in range(DEVICES)]
    return lax.ppermute(block, AXES, route)


def along_x_lo(block):
    return move(block, lambda xh, xl, y, z, c: (xh, 1 - xl, y, z, c))


def along_x_hi(block):
    return move(block, lambda xh, xl, y, z, c: (1 - xh, xl, y, z, c))


def along_y(block, n):
    return move(block, lambda xh, xl, y, z, c: (xh, xl, y + n, z, c))


def along_z(block, n):
    return move(block, lambda xh, xl, y, z, c: (xh, xl, y, z + n, c))


def other_core(block):
    return move(block, lambda xh, xl, y, z, c: (xh, xl, y, z, 1 - c))


def together(*blocks):
    return lax.optimization_barrier(blocks)


def pair_in_plane(turn, y):
    return 2 * (turn // 2 ^ y // 2) + (turn % 2 ^ y % 2)


def to_row_owner(block, turn):
    def step(xh, xl, y, z, c):
        pair = pair_in_plane(turn, y)
        return xh ^ pair % 2 ^ xl, pair % 2, 2 * xh + pair // 2, z, c

    return move(block, step)


def split(x):
    high = x.astype(jnp.bfloat16)
    return high, (x - high.astype(jnp.float32)).astype(jnp.bfloat16)


def columns_kernel(sizes, skip, first, facts_ref, *refs):
    n = len(sizes)
    pieces, refs = refs[:n], refs[n:]
    if first:
        high_out, low_out, centre_out, sums_out, high, low, sems = refs
    else:
        centre_in, sums_in, _, _, high_out, low_out, sums_out, high, low, sems = refs
    size = sizes[0]
    copies = []
    for i in range(n):
        block = pieces[i][...]
        if first and i == 0:
            centre = jnp.sum(block, axis=0, keepdims=True) / size
            centre_out[...] = centre
            sums = jnp.zeros_like(centre)
        elif i == 0:
            centre, sums = centre_in[...], sums_in[...]
        block = block - centre
        sums = sums + jnp.sum(block, axis=0, keepdims=True)
        high[i], low[i] = split(block)
        there = pl.ds(pl.multiple_of(facts_ref[FACTS["order"] + skip + i] * size, size), size)
        for j, (held, out) in enumerate(((high, high_out), (low, low_out))):
            copy = pltpu.make_async_copy(held.at[i], out.at[there], sems.at[2 * i + j])
            copy.start()
            copies.append(copy)
    sums_out[...] = sums
    for copy in copies:
        copy.wait()


def split_columns(pieces, skip, facts, total, state=None):
    sizes = [p.shape[0] for p in pieces]
    width = pieces[0].shape[1]
    n, first = len(pieces), state is None
    whole = jax.ShapeDtypeStruct((total, width), jnp.bfloat16)
    line = jax.ShapeDtypeStruct((1, width), jnp.float32)
    anywhere = pl.BlockSpec(memory_space=SPACE)
    held = pl.BlockSpec(memory_space=pltpu.VMEM)
    more, more_specs, aliases = [], [], {}
    if not first:
        high, low, centre, sums = state
        more, more_specs = [centre, sums, high, low], [held, held, anywhere, anywhere]
        aliases = {n + 3: 0, n + 4: 1}
    count = sum(sizes) * width
    out = pl.pallas_call(
        functools.partial(columns_kernel, sizes, skip, first),
        grid_spec=pltpu.PrefetchScalarGridSpec(
            num_scalar_prefetch=1,
            grid=(),
            in_specs=[held] * n + more_specs,
            out_specs=[anywhere, anywhere] + [held] * (2 if first else 1),
            scratch_shapes=[
                pltpu.VMEM((n, sizes[0], width), jnp.bfloat16),
                pltpu.VMEM((n, sizes[0], width), jnp.bfloat16),
                pltpu.SemaphoreType.DMA((2 * n,)),
            ],
        ),
        out_shape=[whole, whole] + [line] * (2 if first else 1),
        input_output_aliases=aliases,
        cost_estimate=pl.CostEstimate(flops=count, bytes_accessed=2 * count, transcendentals=0),
        compiler_params=pltpu.CompilerParams(vmem_limit_bytes=VMEM),
        name="split_columns",
    )(facts, *pieces, *more)
    if first:
        return out
    return out[0], out[1], state[2], out[2]


def start_columns(facts_ref, pairs, sources, held, sems):
    copies = []
    size = held[0].shape[1] // 2
    for n, pair in enumerate(pairs):
        for i in range(2):
            row = facts_ref[FACTS["order"] + 2 * pair + i] * size
            for j in range(2):
                copies.append(
                    pltpu.make_async_copy(
                        sources[j].at[pl.ds(pl.multiple_of(row, size), size)],
                        held[j].at[n, pl.ds(i * size, size)],
                        sems.at[4 * n + 2 * i + j],
                    )
                )
                copies[-1].start()
    return copies


def write_out(facts_ref, total, edge, sums, count, outs, done, parts, sems):
    rows = total.shape[0] // 4
    done[0] = total[: 2 * rows] / count
    done[1] = (total[2 * rows :] - edge * (sums / count)) / (count - LAG)
    copies = []
    for i, out in enumerate(outs):
        for half in range(2):
            there = out.at[half, facts_ref[FACTS["chunks"] + parts]]
            here = done.at[i, pl.ds(half * rows, rows)]
            copies.append(pltpu.make_async_copy(here, there, sems.at[2 * i + half]))
            copies[-1].start()
    return copies


dot = functools.partial(jnp.dot, preferred_element_type=jnp.float32)


def chunk_kernel(part, ready, facts_ref, *refs):
    last = ready == 4
    pieces, (bh_in, bl_in), refs = refs[:4], refs[4:6], refs[6:]
    if last:
        sums, _, _, instant_out, lagged_out, held, bh, bl, total, done, sems = refs
    else:
        total, edge_out, high_out, low_out, held, bh, bl, sems = refs
    groups, rows, frames = pieces[0].shape

    b_copies = start_columns(facts_ref, range(ready), (bh_in, bl_in), (bh, bl), sems.at[pl.ds(4, 16)])

    for half in range(2):
        sum_ = jnp.zeros((rows, frames), jnp.float32)
        for g in range(groups):
            sum_ = sum_ + (pieces[2 * half][g] + pieces[2 * half + 1][g])
        mean = jnp.sum(sum_, axis=1, keepdims=True) / (2 * groups * frames)
        core = facts_ref[FACTS["core"]]
        core = core if half == 0 else 1 - core
        there = pl.ds(pl.multiple_of(core * rows, rows), rows)
        for i in range(2):
            for g in range(groups):
                held[facts_ref[FACTS["times"] + 2 * g + i], there, :] = pieces[2 * half + i][g] - mean

    edge = jnp.zeros((2 * rows, 1), jnp.float32)
    lane = lax.broadcasted_iota(jnp.int32, (2 * rows, frames), 1)
    for pair in range(4):
        now, shifted = [], []
        for i in range(2):
            time = facts_ref[FACTS["order"] + 2 * pair + i]
            now.append(held[time])
            before = held[jnp.maximum(time - 1, 0)]
            before = jnp.where(time == 0, 0.0, before)
            moved = jnp.where(lane < LAG, pltpu.roll(before, LAG, 1), pltpu.roll(now[i], LAG, 1))
            edge = edge + jnp.sum(moved, axis=1, keepdims=True)
            shifted.append(moved)
        both = [jnp.concatenate(blocks, axis=1) for blocks in (now, shifted)]
        high, low = split(jnp.concatenate(both, axis=0))
        if pair >= ready:
            high_out[pair - ready], low_out[pair - ready] = high, low
            continue
        for copy in b_copies[4 * pair : 4 * pair + 4]:
            copy.wait()
        product = dot(high, bh[pair]) + dot(low, bh[pair]) + dot(high, bl[pair])
        if pair == 0:
            total[...] = product
        else:
            total[...] += product
    if last:
        copies = write_out(
            facts_ref, total, edge, sums[...], 2 * groups * frames, (instant_out, lagged_out), done, part, sems
        )
        for copy in copies:
            copy.wait()
    else:
        edge_out[...] = jnp.broadcast_to(edge, edge_out.shape)


def finish_kernel(parts, facts_ref, *refs):
    n = len(parts)
    begun, refs = refs[: 4 * n], refs[4 * n :]
    far, cross_far, centre, sums_in, bh_in, bl_in, instant_out, lagged_out, bh_out, bl_out, sums_out = refs[:11]
    bh, bl, done, sems = refs[11:]
    copies, sums = [], sums_in[...]
    for i, piece in enumerate((far, cross_far)):
        size = piece.shape[0]
        block = piece[...] - centre[...]
        sums = sums + jnp.sum(block, axis=0, keepdims=True)
        here = pl.ds(i * size, size)
        bh[here], bl[here] = split(block)
        there = pl.ds(pl.multiple_of(facts_ref[FACTS["order"] + 6 + i] * size, size), size)
        for j, (held, out) in enumerate(((bh, bh_out), (bl, bl_out))):
            copies.append(pltpu.make_async_copy(held.at[here], out.at[there], sems.at[4 * n + 2 * i + j]))
            copies[-1].start()
    sums_out[...] = sums
    for i in range(n):
        total, edge, high, low = begun[4 * i : 4 * i + 4]
        last = high.shape[0] - 1
        now = total[...] + (dot(high[last], bh[...]) + dot(low[last], bh[...]) + dot(high[last], bl[...]))
        count = 4 * high.shape[2]
        copies += write_out(
            facts_ref, now, edge[:, :1], sums, count, (instant_out, lagged_out), done.at[i], parts[i], sems.at[pl.ds(4 * i, 4)]
        )
    for copy in copies:
        copy.wait()


def begin(part, ready, pieces, columns, facts):
    bh, bl = columns[:2]
    groups, rows, frames = pieces[0].shape
    width, run = bh.shape[1], 2 * frames
    anywhere = pl.BlockSpec(memory_space=SPACE)
    held = pl.BlockSpec(memory_space=pltpu.VMEM)
    return pl.pallas_call(
        functools.partial(chunk_kernel, part, ready),
        grid_spec=pltpu.PrefetchScalarGridSpec(
            num_scalar_prefetch=1,
            grid=(),
            in_specs=[held] * 4 + [anywhere] * 2,
            out_specs=[held] * 4,
            scratch_shapes=[
                pltpu.VMEM((SLOTS, 2 * rows, frames), jnp.float32),
                pltpu.VMEM((ready, run, width), jnp.bfloat16),
                pltpu.VMEM((ready, run, width), jnp.bfloat16),
                pltpu.SemaphoreType.DMA((20,)),
            ],
        ),
        out_shape=[
            jax.ShapeDtypeStruct((4 * rows, width), jnp.float32),
            jax.ShapeDtypeStruct((2 * rows, 128), jnp.float32),
            jax.ShapeDtypeStruct((4 - ready, 4 * rows, run), jnp.bfloat16),
            jax.ShapeDtypeStruct((4 - ready, 4 * rows, run), jnp.bfloat16),
        ],
        cost_estimate=pl.CostEstimate(
            flops=rows * ready * run * width, bytes_accessed=groups * run * (2 * rows + width), transcendentals=0
        ),
        compiler_params=pltpu.CompilerParams(vmem_limit_bytes=VMEM),
        name="begin",
    )(facts, *pieces, bh, bl)


def advance_kernel(facts_ref, total, high, low, bh_in, bl_in, out, bh, bl, sems):
    copies = start_columns(facts_ref, [2], (bh_in, bl_in), (bh, bl), sems)
    for copy in copies:
        copy.wait()
    out[...] = total[...] + (dot(high[0], bh[0]) + dot(low[0], bh[0]) + dot(high[0], bl[0]))


def advance(begun, columns, facts):
    total, edge, high, low = begun
    bh, bl = columns[:2]
    width, run = bh.shape[1], high.shape[2]
    anywhere = pl.BlockSpec(memory_space=SPACE)
    held = pl.BlockSpec(memory_space=pltpu.VMEM)
    total = pl.pallas_call(
        advance_kernel,
        grid_spec=pltpu.PrefetchScalarGridSpec(
            num_scalar_prefetch=1,
            grid=(),
            in_specs=[held] * 3 + [anywhere] * 2,
            out_specs=held,
            scratch_shapes=[
                pltpu.VMEM((1, run, width), jnp.bfloat16),
                pltpu.VMEM((1, run, width), jnp.bfloat16),
                pltpu.SemaphoreType.DMA((4,)),
            ],
        ),
        out_shape=jax.ShapeDtypeStruct(total.shape, total.dtype),
        cost_estimate=pl.CostEstimate(
            flops=total.shape[0] * run * width, bytes_accessed=run * (total.shape[0] + width), transcendentals=0
        ),
        compiler_params=pltpu.CompilerParams(vmem_limit_bytes=VMEM),
        name="advance",
    )(facts, total, high, low, bh, bl)
    return total, edge, high, low


def finish(parts, begun, far, cross_far, columns, facts):
    bh, bl, centre, sums = columns
    rows, width = begun[0][1].shape[0] // 2, bh.shape[1]
    run = begun[0][2].shape[2]
    anywhere = pl.BlockSpec(memory_space=SPACE)
    held = pl.BlockSpec(memory_space=pltpu.VMEM)
    shape = jax.ShapeDtypeStruct((2, 4, rows, width), jnp.float32)
    n = len(parts)
    *outs, bh, bl, sums = pl.pallas_call(
        functools.partial(finish_kernel, parts),
        grid_spec=pltpu.PrefetchScalarGridSpec(
            num_scalar_prefetch=1,
            grid=(),
            in_specs=[held] * (4 * n + 4) + [anywhere] * 2,
            out_specs=[anywhere] * 4 + [held],
            scratch_shapes=[
                pltpu.VMEM((run, width), jnp.bfloat16),
                pltpu.VMEM((run, width), jnp.bfloat16),
                pltpu.VMEM((n, 2, 2 * rows, width), jnp.float32),
                pltpu.SemaphoreType.DMA((4 * n + 4,)),
            ],
        ),
        out_shape=[shape, shape, *(jax.ShapeDtypeStruct(x.shape, x.dtype) for x in (bh, bl, sums))],
        input_output_aliases={4 * n + 5: 2, 4 * n + 6: 3},
        cost_estimate=pl.CostEstimate(
            flops=2 * 3 * 4 * rows * n * run * width, bytes_accessed=4 * n * (4 * rows * run + 8 * rows * width), transcendentals=0
        ),
        compiler_params=pltpu.CompilerParams(vmem_limit_bytes=VMEM),
        name="finish",
    )(facts, *(array for chunk in begun for array in chunk), far, cross_far, centre, sums, bh, bl)
    return outs, (bh, bl, centre, sums)


def whole(part, pieces, columns, facts, outs):
    bh, bl, _, sums = columns
    groups, rows, frames = pieces[0].shape
    width, run = bh.shape[1], 2 * frames
    anywhere = pl.BlockSpec(memory_space=SPACE)
    held = pl.BlockSpec(memory_space=pltpu.VMEM)
    shape = jax.ShapeDtypeStruct((2, 4, rows, width), jnp.float32)
    return pl.pallas_call(
        functools.partial(chunk_kernel, part, 4),
        grid_spec=pltpu.PrefetchScalarGridSpec(
            num_scalar_prefetch=1,
            grid=(),
            in_specs=[held] * 4 + [anywhere] * 2 + [held] + [anywhere] * 2,
            out_specs=[anywhere, anywhere],
            scratch_shapes=[
                pltpu.VMEM((SLOTS, 2 * rows, frames), jnp.float32),
                pltpu.VMEM((4, run, width), jnp.bfloat16),
                pltpu.VMEM((4, run, width), jnp.bfloat16),
                pltpu.VMEM((4 * rows, width), jnp.float32),
                pltpu.VMEM((2, 2 * rows, width), jnp.float32),
                pltpu.SemaphoreType.DMA((20,)),
            ],
        ),
        out_shape=[shape, shape],
        input_output_aliases={8: 0, 9: 1},
        cost_estimate=pl.CostEstimate(
            flops=2 * 3 * 4 * rows * groups * run * width, bytes_accessed=4 * groups * run * (2 * rows + width), transcendentals=0
        ),
        compiler_params=pltpu.CompilerParams(vmem_limit_bytes=VMEM),
        name="whole",
    )(facts, *pieces, bh, bl, sums, *outs)


def on_device(frames):
    rows, width = frames.shape
    quarter = width // 4
    total = SLOTS * rows
    tm, feat = lax.axis_index("tm"), lax.axis_index("feat")
    y, x_lo, x_hi, z, core = tm // 2, tm % 2, feat // 8, feat // 2 % 4, feat % 2

    quarters = frames.T.reshape(4, quarter, rows)
    spread = [quarters[0]] + [along_z(quarters[n], n) for n in (1, 2, 3)]
    cross = along_x_lo(frames)
    landed = []
    for turn in range(4):
        which = lax.rem(z - pair_in_plane(turn, y) + 4, 4)
        piece = lax.select_n(which, *spread)
        if turn in (0, 1):
            piece, cross = together(piece, cross)
        landed.append(to_row_owner(piece, turn))
    *landed, frames = together(*landed, frames)
    landed = jnp.stack(landed)
    swapped = along_x_hi(landed)
    landed_below, landed_above = along_z(landed, 1), along_z(landed, -1)
    below, above = along_y(frames, 1), along_y(frames, -1)
    landed_other = other_core(landed)
    swapped, landed_below, landed_above, below, above, cross, landed_other = together(
        swapped, landed_below, landed_above, below, above, cross, landed_other
    )

    x_first = x_hi ^ y // 2 ^ x_lo
    runs = [2 * (y % 2 ^ turn // 2) + (x_lo ^ turn % 2) for turn in range(4)]
    times = [2 * run + x for run in runs for x in (x_first, 1 - x_first)]

    def block(away, x_from):
        return lax.rem(y + away + 4, 4) * 2 + x_from

    here, there = x_lo, 1 - x_lo
    order = [block(0, here), block(0, there), block(-1, here), block(1, here)]
    order += [block(-1, there), block(1, there), block(2, here), block(2, there)]
    first = z - (y % 2 * 2 + x_lo)
    chunks = [lax.rem(first + away + 8, 4) for away in (0, -1, 1, 2)]
    facts = jnp.stack([core, *times, *order, *chunks]).astype(jnp.int32)

    swapped_below, swapped_above = along_z(swapped, 1), along_z(swapped, -1)
    cross_below, cross_above = along_y(cross, 1), along_y(cross, -1)
    swapped_other = other_core(swapped)
    columns1 = split_columns([frames, cross, below, above], 0, facts, total)
    begun = [begin(0, 2, (landed, swapped, landed_other, swapped_other), columns1, facts)]
    early_below, early_above, _ = together(landed_below, landed_above, begun[0][1])
    below_other, above_other = other_core(early_below), other_core(early_above)
    swapped_below, swapped_above, cross_below, cross_above, landed_below, below, below_other, above_other = together(
        swapped_below, swapped_above, cross_below, cross_above, landed_below, below, below_other, above_other
    )

    landed_far, swapped_far = along_z(landed_below, 1), along_z(swapped_above, -1)
    far, cross_far = along_y(below, 1), along_y(cross_above, -1)
    columns2 = split_columns([cross_below, cross_above], 4, facts, total, columns1)
    begun.append(begin(1, 3, (landed_below, swapped_below, below_other, other_core(swapped_below)), columns2, facts))
    begun.append(begin(2, 3, (landed_above, swapped_above, above_other, other_core(swapped_above)), columns2, facts))
    begun[0] = advance(begun[0], columns2, facts)
    landed_far, swapped_far, *_ = together(landed_far, swapped_far, begun[0][0], begun[1][1], begun[2][1])
    outs, columns3 = finish(range(3), begun, far, cross_far, columns2, facts)
    far_other = other_core(landed_far), other_core(swapped_far)
    outs = whole(3, (landed_far, swapped_far, *far_other), columns3, facts, outs)
    return tuple(out.reshape(2 * width, width) for out in outs)


def solution(mesh):
    return jax.shard_map(
        on_device,
        mesh=mesh,
        in_specs=(P("tm", "feat"),),
        out_specs=(P("tm", "feat"), P("tm", "feat")),
        check_vma=False,
    )
```
